128 devices in a mesh: dp: 16 (over y, z), seq: 8 (over x, core).
Axes of the slice: x: 4, y: 4, z: 4, core: 2. Of those that a mesh axis runs over, the one named last changes fastest.
Arguments:
- queries: bfloat16 [16, 2048, 2048], P('dp', 'seq'), may hold values from -4.5 to 4.5
- key_states: bfloat16 [16, 2048, 2048], P('dp', 'seq'), may hold values from -4.5 to 4.5
- value_states: bfloat16 [16, 2048, 2048], P('dp', 'seq'), may hold values from -6 to 6
- grad_output: bfloat16 [16, 2048, 2048], P('dp', 'seq'), may hold values from -6 to 6
- out_weight: bfloat16 [2048, 2048], P('dp'), may hold values from -0.125 to 0.125
- key_tiles: int32 [16, 16, 16, 7], P('dp'), may hold values from 0 to 15, as said below
- tile_count: int32 [16, 16, 16], P('dp'), may hold values from 1 to 7, as said below
Outputs:
- output: bfloat16 [16, 2048, 2048], P('dp', 'seq')
- grad_query: bfloat16 [16, 2048, 2048], P('dp', 'seq')
- grad_key: bfloat16 [16, 2048, 2048], P('dp', 'seq')
- grad_value: bfloat16 [16, 2048, 2048], P('dp', 'seq')
- grad_weight: float32 [2048, 2048], P('dp')
The draws below stay inside these ranges and needn't reach their ends.
Inputs may be any that keep to these rules, and one draw needn't show every extreme that they name: `key_tiles`: entry 0 of every list is the query tile itself; the first tile_count entries of a list are distinct tiles, the others are ignored. For every clip and query tile, tile_count of head h plus tile_count of head h + 8 is exactly 8.
All inputs are finite; a program needn't handle non-finite values.
Results may differ from the reference program's by a relative error of at most 0.024.
Values may be sent and summed in bfloat16 or wider, within the bound.
No kernel may reach another device: no remote copies, remote signals or barrier semaphores. Data moves between devices by JAX's collectives and lax.ppermute only.
A program may use at most 192 MiB of HBM per device.

```python
import math
import jax
import jax.numpy as jnp
from jax import lax

D = 2048
HEADS = 16
HEAD_DIM = 128
KMAX = 7
CLIPS = 16
LENGTH = 2048
QTILES = 16


def mask_plan(key):

    def one_clip(clip_number):
        clip_key = jax.random.fold_in(key, clip_number)
        part_keys = jax.random.split(clip_key, 5)
        couples = HEADS // 2
        flips = jax.random.randint(part_keys[0], (couples,), 0, 2)
        first_heads = jnp.arange(couples)
        heavy_heads = first_heads + flips * couples
        light_heads = first_heads + (1 - flips) * couples
        shifts = jax.random.randint(part_keys[2], (couples, QTILES), 0, 3)
        forced = jax.random.randint(part_keys[3], (couples,), 0, QTILES)
        shifts = jnp.where(jnp.arange(QTILES)[None, :] == forced[:, None], 0, shifts)
        counts = jnp.zeros((HEADS, QTILES), jnp.int32).at[heavy_heads].set(KMAX - shifts).at[light_heads].set(1 + shifts)
        rank_table = jax.random.randint(part_keys[4], (HEADS, QTILES, QTILES), 0, QTILES) * QTILES + jnp.arange(QTILES)[None, None, :]
        own_tile = jnp.arange(QTILES)[None, :, None] == jnp.arange(QTILES)[None, None, :]
        rank_table = jnp.where(own_tile, -1, rank_table)
        tile_lists = jnp.argsort(rank_table, axis=-1)[:, :, :KMAX].astype(jnp.int32)
        return (tile_lists, counts.astype(jnp.int32))
    return jax.vmap(one_clip)(jnp.arange(CLIPS))


def draw_queries(key, part):
    key = jax.random.fold_in(key, 1)
    base_draw = jnp.clip(jax.random.normal(key, (CLIPS, LENGTH, HEADS, HEAD_DIM), jnp.float32), -4.5, 4.5)
    return base_draw.reshape(CLIPS, LENGTH, HEADS * HEAD_DIM).astype(jnp.bfloat16)


def draw_key_states(key, part):
    key = jax.random.fold_in(key, 2)
    base_draw = jnp.clip(jax.random.normal(key, (CLIPS, LENGTH, HEADS, HEAD_DIM), jnp.float32), -4.5, 4.5)
    return base_draw.reshape(CLIPS, LENGTH, HEADS * HEAD_DIM).astype(jnp.bfloat16)


def draw_key_tiles(key, part):
    tables = mask_plan(key)
    return tables[0]


def draw_tile_count(key, part):
    tables = mask_plan(key)
    return tables[1]


def spiked(result, key, source, target, parts, factor):
    def block_of(dim):
        return (jnp.arange(result.shape[dim]) // (result.shape[dim] // parts)).reshape((-1,) + (1,) * (result.ndim - 1 - dim))

    near = jax.random.permutation(key, parts)[block_of(target)]
    other_side = (block_of(target) + parts // 2) % parts
    return jnp.where((block_of(source) == near) | (block_of(source) == other_side), factor * result, result)


def steps_of(stream_key, extent, pieces, least, top_value):
    def one(position, shards_of):
        draws = jax.random.uniform(jax.random.fold_in(jax.random.fold_in(stream_key, 6), position), (shards_of,), jnp.float32, least / len(pieces), top_value / len(pieces))
        return jnp.repeat(jnp.exp(draws), extent[position] // shards_of).reshape((-1,) + (1,) * (len(extent) - position - 1))

    level = one(*pieces[0])
    for cut in pieces[1:]:
        level = level * one(*cut)
    return level


def bell_draw(stream_key, dims, width, bound, cuts=(), dtype=jnp.bfloat16):
    entries = jax.random.normal(stream_key, dims, jnp.float32) * width
    if len(cuts) > 0:
        entries = steps_of(stream_key, dims, cuts, -0.22, 0.18) * entries
    return jnp.clip(entries, min=-bound, max=bound).astype(dtype)


def noise_with(key, shape, spread, limit, shards, heavy, dtype=jnp.bfloat16):
    values = spread * jax.random.normal(key, shape, jnp.float32)
    if shards:
        values = values * steps_of(key, shape, shards, -0.22, 0.18)
    return jnp.clip(spiked(values, jax.random.fold_in(key, 3), *heavy), -limit, limit).astype(dtype)


def setup_inputs(seed: int = 0) -> dict:
    keys = jax.random.split(jax.random.key(seed), 8)
    return {
        "queries": draw_queries(jax.random.fold_in(keys[7], 71), 0),
        "key_states": draw_key_states(jax.random.fold_in(keys[7], 71), 0),
        "value_states": bell_draw(keys[2], (CLIPS, LENGTH, HEADS * HEAD_DIM), 1.0, 6.0, ((0, 16), (1, 8))),
        "grad_output": noise_with(keys[3], (CLIPS, LENGTH, D), 1.0, 6.0, ((0, 16), (1, 8)), (1, 2, 8, 2.0)),
        "out_weight": bell_draw(keys[4], (D, HEADS * HEAD_DIM), (HEADS * HEAD_DIM) ** -0.5, 0.125, ((0, 16),)),
        "key_tiles": draw_key_tiles(jax.random.fold_in(keys[7], 71), 0),
        "tile_count": draw_tile_count(jax.random.fold_in(keys[7], 71), 0),
    }


def rounded(values):
    return lax.optimization_barrier(values.astype(jnp.bfloat16)).astype(jnp.float32)

def head_pass(bundle):
    q_head, k_head, v_head, g_head, tile_lists, counts = bundle
    tile_total = counts.shape[0]
    list_width = tile_lists.shape[1]
    head_dim = q_head.shape[-1]
    score_scale = 1.0 / math.sqrt(head_dim)
    q_units = q_head.reshape(tile_total, -1, head_dim).astype(jnp.float32)
    tile_rows = q_units.shape[1]
    k_tiles = k_head.reshape(tile_total, tile_rows, head_dim)
    v_tiles = v_head.reshape(tile_total, tile_rows, head_dim)
    k_chosen = k_tiles[tile_lists].reshape(tile_total, list_width * tile_rows, head_dim).astype(jnp.float32)
    v_chosen = v_tiles[tile_lists].reshape(tile_total, list_width * tile_rows, head_dim).astype(jnp.float32)
    g_units = g_head.reshape(tile_total, tile_rows, head_dim).astype(jnp.float32)
    valid = jnp.repeat(jnp.arange(list_width)[None, :] < counts[:, None], tile_rows, axis=1)[:, None, :]
    scores = jnp.einsum('urd,usd->urs', q_units, k_chosen) * score_scale
    row_top = lax.optimization_barrier(jnp.max(jnp.where(valid, scores, -jnp.inf), axis=-1))
    probabilities = jnp.where(valid, jnp.exp(scores - row_top[:, :, None]), 0.0)
    row_total = lax.optimization_barrier(jnp.sum(probabilities, axis=-1))
    mixed_rows = jnp.einsum('urs,usd->urd', rounded(probabilities), v_chosen)
    attention = (mixed_rows / row_total[:, :, None]).astype(jnp.bfloat16)
    log_total = row_top + jnp.log(row_total)
    row_delta = lax.optimization_barrier(jnp.sum(g_units * attention.astype(jnp.float32), axis=-1))
    replayed = jnp.where(valid, jnp.exp(scores - log_total[:, :, None]), 0.0)
    value_parts = jnp.einsum('urs,urd->usd', rounded(replayed), g_units)
    grad_prob = jnp.einsum('urd,usd->urs', g_units, v_chosen)
    grad_score = rounded(replayed * (grad_prob - row_delta[:, :, None]))
    grad_query = (jnp.einsum('urs,usd->urd', grad_score, k_chosen) * score_scale).astype(jnp.bfloat16)
    key_parts = jnp.einsum('urs,urd->usd', grad_score, q_units) * score_scale
    segment_ids = tile_lists.reshape(-1).astype(jnp.int32)
    grad_key = jax.ops.segment_sum(key_parts.reshape(tile_total * list_width, tile_rows, head_dim), segment_ids, tile_total)
    grad_value = jax.ops.segment_sum(value_parts.reshape(tile_total * list_width, tile_rows, head_dim), segment_ids, tile_total)
    return (attention.reshape(-1, head_dim), grad_query.reshape(-1, head_dim), grad_key.reshape(-1, head_dim).astype(jnp.bfloat16), grad_value.reshape(-1, head_dim).astype(jnp.bfloat16))

def reference(queries, key_states, value_states, grad_output, out_weight, key_tiles, tile_count):
    head_count = tile_count.shape[1]
    length = queries.shape[1]
    columns = queries.shape[2]
    head_dim = columns // head_count

    def by_head(values):
        return values.reshape(length, head_count, head_dim).transpose(1, 0, 2)

    def joined(values):
        return values.transpose(1, 0, 2).reshape(length, columns)

    def clip_pass(weight_sum, bundle):
        q_clip, k_clip, v_clip, dy_clip, lists_clip, counts_clip = bundle
        grad_attn = jnp.dot(dy_clip, out_weight, preferred_element_type=jnp.float32).astype(jnp.bfloat16)
        results = lax.map(head_pass, (by_head(q_clip), by_head(k_clip), by_head(v_clip), by_head(grad_attn), lists_clip, counts_clip))
        attention = joined(results[0])
        output = jnp.dot(attention, out_weight.T, preferred_element_type=jnp.float32).astype(jnp.bfloat16)
        weight_sum = weight_sum + jnp.dot(dy_clip.T, attention, preferred_element_type=jnp.float32)
        return (weight_sum, (output, joined(results[1]), joined(results[2]), joined(results[3])))
    initial = jnp.zeros((out_weight.shape[0], columns), jnp.float32)
    grad_weight, stacked = lax.scan(clip_pass, initial, (queries, key_states, value_states, grad_output, key_tiles, tile_count))
    return (stacked[0], stacked[1], stacked[2], stacked[3], grad_weight)
```

```python
import functools
import math

import jax
import jax.numpy as jnp
from jax import lax
from jax.experimental import pallas as pl
from jax.experimental.pallas import tpu as pltpu
from jax.sharding import PartitionSpec as P

NN = (((1,), (0,)), ((), ()))
NT = (((1,), (1,)), ((), ()))
TN = (((0,), (0,)), ((), ()))
F32 = jnp.float32
BF16 = jnp.bfloat16
MIB = 2**20
SMEM = pl.BlockSpec(memory_space=pltpu.SMEM)
VMEM = pl.BlockSpec(memory_space=pltpu.VMEM)
ANY = pl.BlockSpec(memory_space=pl.ANY)
TILE = 128


def mm(a, b, dims=NN):
    return lax.dot_general(a, b, dims, preferred_element_type=F32)


def cost(flops, moved, exps=0):
    return pl.CostEstimate(flops=flops, bytes_accessed=moved, transcendentals=exps)


def pack_kernel(q_ref, k_ref, v_ref, out_ref, sems):
    seq, _, halves, _, width = out_ref.shape
    copies = []
    for n, ref in enumerate((q_ref, k_ref, v_ref)):
        for s in range(seq):
            for half in range(halves):
                source = ref.at[0, :, pl.ds((s + seq * half) * width, width)]
                copies.append(pltpu.make_async_copy(source, out_ref.at[s, n, half], sems.at[len(copies)]))
    for copy in copies:
        copy.start()
    for copy in copies:
        copy.wait()


def pack(q, k, v, seq, head_dim):
    _, tokens, columns = q.shape
    halves = columns // (seq * head_dim)
    return pl.pallas_call(
        pack_kernel,
        out_shape=jax.ShapeDtypeStruct((seq, 3, halves, tokens, head_dim), q.dtype),
        in_specs=[ANY] * 3,
        out_specs=ANY,
        scratch_shapes=[pltpu.SemaphoreType.DMA((3 * seq * halves,))],
        cost_estimate=cost(0, 12 * tokens * columns),
        name="pack_heads",
    )(q, k, v)


def unpack_kernel(in_ref, q_ref, k_ref, v_ref, sems):
    seq, _, halves, _, width = in_ref.shape
    copies = []
    for n, ref in enumerate((q_ref, k_ref, v_ref)):
        for s in range(seq):
            for half in range(halves):
                target = ref.at[0, :, pl.ds((s + seq * half) * width, width)]
                copies.append(pltpu.make_async_copy(in_ref.at[s, n, half], target, sems.at[len(copies)]))
    for copy in copies:
        copy.start()
    for copy in copies:
        copy.wait()


def unpack(blocks):
    seq, _, halves, tokens, head_dim = blocks.shape
    columns = seq * halves * head_dim
    return pl.pallas_call(
        unpack_kernel,
        out_shape=(jax.ShapeDtypeStruct((1, tokens, columns), blocks.dtype),) * 3,
        in_specs=[ANY],
        out_specs=(ANY,) * 3,
        scratch_shapes=[pltpu.SemaphoreType.DMA((3 * seq * halves,))],
        cost_estimate=cost(0, 12 * tokens * columns),
        name="unpack_heads",
    )(blocks)


def slot_plan(place_ref, tiles_ref, counts_ref, unit, slot, units, width):
    first_head = place_ref[0]
    split = counts_ref[first_head * units + unit]
    in_first = slot < split
    head = jnp.where(in_first, first_head, first_head + place_ref[1])
    entry = jnp.minimum(jnp.where(in_first, slot, width - slot), width - 1)
    tile = tiles_ref[(head * units + unit) * width + entry]
    return in_first, jnp.where(in_first, 0, 1), tile


def rows_of(ref, half, tile):
    per_block = ref.shape[2] // TILE
    start = pl.multiple_of(lax.rem(tile, per_block) * TILE, TILE)
    return ref.at[lax.div(tile, per_block), half, pl.ds(start, TILE), :]


def forward_kernel(slots, units, width, scale, place_ref, tiles_ref, counts_ref, qkv_ref, a_ref, lse_ref, vt_ref, s_ref, p_ref):
    scale2 = scale * math.log2(math.e)
    q_ref, k_ref, v_ref = (qkv_ref.at[:, n] for n in range(3))

    @pl.loop(0, units)
    def _(t):
        for half in range(2):
            vt_ref[half * units + t] = rows_of(v_ref, half, t)[...].T

    @pl.loop(0, units)
    def _(unit):
        plans = [slot_plan(place_ref, tiles_ref, counts_ref, unit, j, units, width) for j in range(slots)]
        tops = []
        for j, (in_first, half, tile) in enumerate(plans):
            q = rows_of(q_ref, half, unit)[...]
            s = mm(rows_of(k_ref, half, tile)[...], q, NT)
            s_ref[j] = s
            tops.append(jnp.max(s.reshape(TILE // 8, 8, TILE), axis=0))
        low = jnp.full((8, TILE), -jnp.inf, F32)
        top = []
        for half in range(2):
            m = low
            for (in_first, _, _), t8 in zip(plans, tops):
                use = in_first if half == 0 else jnp.logical_not(in_first)
                m = jnp.maximum(m, jnp.where(use, t8, low))
            top.append(jnp.max(m, axis=0, keepdims=True) * scale2)
        totals = [jnp.zeros((8, TILE), F32)] * 2
        zero = jnp.zeros((TILE, TILE), BF16)
        for j, (in_first, half, tile) in enumerate(plans):
            p = jnp.exp2(s_ref[j] * scale2 - jnp.where(in_first, top[0], top[1]))
            l8 = jnp.sum(p.reshape(TILE // 8, 8, TILE), axis=0)
            totals[0] = totals[0] + jnp.where(in_first, l8, 0.0)
            totals[1] = totals[1] + jnp.where(in_first, 0.0, l8)
            pb = p.astype(BF16)
            p_ref[pl.ds(j * TILE, TILE), 0:TILE] = jnp.where(in_first, pb, zero)
            p_ref[pl.ds(j * TILE, TILE), TILE : 2 * TILE] = jnp.where(in_first, zero, pb)
        vt = jnp.concatenate([vt_ref[half * units + tile] for _, half, tile in plans], axis=1)
        mixed = mm(vt, p_ref[...])
        for half in range(2):
            total = jnp.sum(totals[half], axis=0, keepdims=True)
            a_t = mixed[:, half * TILE : (half + 1) * TILE] / total
            rows_of(a_ref, half, unit)[...] = a_t.T.astype(BF16)
            lse_ref[half * units + unit] = jnp.broadcast_to(top[half] + jnp.log2(total), (8, TILE))


def attention_forward(place, tiles, counts, qkv, chips, width):
    seq, _, halves, tokens, head_dim = qkv.shape
    units = seq * tokens // TILE
    slots = width + 1
    return pl.pallas_call(
        functools.partial(forward_kernel, slots, units, width, 1.0 / math.sqrt(head_dim)),
        out_shape=(
            jax.ShapeDtypeStruct((chips, halves, seq * tokens // chips, head_dim), BF16),
            jax.ShapeDtypeStruct((halves * units, 8, TILE), F32),
        ),
        in_specs=[SMEM] * 3 + [VMEM],
        out_specs=(VMEM, VMEM),
        scratch_shapes=[
            pltpu.VMEM((halves * units, head_dim, TILE), BF16),
            pltpu.VMEM((slots, TILE, TILE), F32),
            pltpu.VMEM((slots * TILE, 2 * TILE), BF16),
        ],
        compiler_params=pltpu.CompilerParams(vmem_limit_bytes=24 * MIB),
        cost_estimate=cost(16 * units * slots * TILE**3, 5 * MIB, units * slots * TILE * TILE),
        name="attention_forward",
    )(place, tiles, counts, qkv)


def backward_kernel(slots, units, width, scale, place_ref, tiles_ref, counts_ref, qkv_ref, g_ref, a_ref, lse_ref, out_ref, kt_ref, dk_acc, dv_acc, d_ref):
    scale2 = scale * math.log2(math.e)
    q_ref, k_ref, v_ref = (qkv_ref.at[:, n] for n in range(3))
    dq_ref, dk_ref, dv_ref = (out_ref.at[:, n] for n in range(3))

    @pl.loop(0, units)
    def _(t):
        for half in range(2):
            kt_ref[half * units + t] = rows_of(k_ref, half, t)[...].T
            dk_acc[half * units + t] = jnp.zeros((TILE, TILE), F32)
            dv_acc[half * units + t] = jnp.zeros((TILE, TILE), F32)

    @pl.loop(0, units)
    def _(unit):
        plans = [slot_plan(place_ref, tiles_ref, counts_ref, unit, j, units, width) for j in range(slots)]
        delta = []
        lse = []
        for half in range(2):
            prod = rows_of(g_ref, half, unit)[...].astype(F32) * rows_of(a_ref, half, unit)[...].astype(F32)
            delta.append(jnp.sum(prod.T, axis=0, keepdims=True))
            lse.append(lse_ref[half * units + unit][0:1])
        zero = jnp.zeros((TILE, TILE), BF16)
        for j, (in_first, half, tile) in enumerate(plans):
            q = rows_of(q_ref, half, unit)[...]
            g = rows_of(g_ref, half, unit)[...]
            s = mm(rows_of(k_ref, half, tile)[...], q, NT)
            p = jnp.exp2(s * scale2 - jnp.where(in_first, lse[0], lse[1]))
            dp = mm(rows_of(v_ref, half, tile)[...], g, NT)
            ds = (p * (dp - jnp.where(in_first, delta[0], delta[1]))).astype(BF16)
            dv_acc[half * units + tile] += mm(p.astype(BF16), g)
            dk_acc[half * units + tile] += mm(ds, q)
            d_ref[pl.ds(j * TILE, TILE), 0:TILE] = jnp.where(in_first, ds, zero)
            d_ref[pl.ds(j * TILE, TILE), TILE : 2 * TILE] = jnp.where(in_first, zero, ds)
        kt = jnp.concatenate([kt_ref[half * units + tile] for _, half, tile in plans], axis=1)
        dq_t = mm(kt, d_ref[...]) * scale
        for half in range(2):
            rows_of(dq_ref, half, unit)[...] = dq_t[:, half * TILE : (half + 1) * TILE].T.astype(BF16)

    @pl.loop(0, units)
    def _(t):
        for half in range(2):
            rows_of(dk_ref, half, t)[...] = (dk_acc[half * units + t] * scale).astype(BF16)
            rows_of(dv_ref, half, t)[...] = dv_acc[half * units + t].astype(BF16)


def attention_backward(place, tiles, counts, qkv, g, a, lse, width):
    seq, _, halves, tokens, head_dim = qkv.shape
    units = seq * tokens // TILE
    slots = width + 1
    return pl.pallas_call(
        functools.partial(backward_kernel, slots, units, width, 1.0 / math.sqrt(head_dim)),
        out_shape=jax.ShapeDtypeStruct(qkv.shape, BF16),
        in_specs=[SMEM] * 3 + [VMEM] * 4,
        out_specs=VMEM,
        scratch_shapes=[
            pltpu.VMEM((halves * units, head_dim, TILE), BF16),
            pltpu.VMEM((halves * units, TILE, head_dim), F32),
            pltpu.VMEM((halves * units, TILE, head_dim), F32),
            pltpu.VMEM((slots * TILE, 2 * TILE), BF16),
        ],
        compiler_params=pltpu.CompilerParams(vmem_limit_bytes=32 * MIB),
        cost_estimate=cost(36 * units * slots * TILE**3, 9 * MIB, units * slots * TILE * TILE),
        name="attention_backward",
    )(place, tiles, counts, qkv, g, a, lse)


def grad_attn_kernel(place_ref, own_ref, other_ref, w_ref, g_ref):
    tokens = own_ref.shape[0]
    core = place_ref[2]
    for ref, slot in ((own_ref, core), (other_ref, 1 - core)):
        g = mm(ref[...], w_ref[...]).astype(BF16)
        start = pl.multiple_of(slot * tokens, tokens)
        for half in range(2):
            g_ref[0, half, pl.ds(start, tokens), :] = g[:, half * TILE : (half + 1) * TILE]


def grad_attn(place, own, other, weights, chips):
    tokens, depth = own.shape
    columns = weights.shape[1]
    block = columns // chips
    return pl.pallas_call(
        grad_attn_kernel,
        grid=(chips,),
        out_shape=jax.ShapeDtypeStruct((chips, 2, 2 * tokens, block // 2), BF16),
        in_specs=[
            SMEM,
            pl.BlockSpec((tokens, depth), lambda i: (0, 0)),
            pl.BlockSpec((tokens, depth), lambda i: (0, 0)),
            pl.BlockSpec((depth, block), lambda i: (0, i)),
        ],
        out_specs=pl.BlockSpec((1, 2, 2 * tokens, block // 2), lambda i: (i, 0, 0, 0)),
        compiler_params=pltpu.CompilerParams(vmem_limit_bytes=24 * MIB),
        cost_estimate=cost(4 * tokens * depth * columns, 7 * MIB),
        name="grad_attn",
    )(place, own, other, weights)


def token_rows(a_ref, slot):
    chips, halves, rows, _ = a_ref.shape
    tokens = rows // 2
    start = pl.multiple_of(slot * tokens, tokens)
    return jnp.concatenate([a_ref[x, half, pl.ds(start, tokens), :] for x in range(chips) for half in range(halves)], axis=1)


def project_kernel(place_ref, a_ref, w_ref, own_ref, other_ref):
    core = place_ref[2]
    own_ref[...] = mm(token_rows(a_ref, core), w_ref[...], NT)
    other_ref[...] = mm(token_rows(a_ref, 1 - core), w_ref[...], NT).astype(BF16)


def project(place, a, weights):
    chips, halves, rows, width = a.shape
    features, columns = weights.shape
    tokens = rows // 2
    block = 256
    return pl.pallas_call(
        project_kernel,
        grid=(features // block,),
        out_shape=(jax.ShapeDtypeStruct((tokens, features), F32), jax.ShapeDtypeStruct((tokens, features), BF16)),
        in_specs=[
            SMEM,
            pl.BlockSpec(a.shape, lambda i: (0, 0, 0, 0)),
            pl.BlockSpec((block, columns), lambda i: (i, 0)),
        ],
        out_specs=(pl.BlockSpec((tokens, block), lambda i: (0, i)), pl.BlockSpec((tokens, block), lambda i: (0, i))),
        compiler_params=pltpu.CompilerParams(vmem_limit_bytes=24 * MIB),
        cost_estimate=cost(4 * tokens * features * columns, 8 * MIB),
        name="project",
    )(place, a, weights)


def grad_weight_kernel(side, place_ref, own_ref, other_ref, a_ref, *out_refs):
    core, y, z = place_ref[2], place_ref[3], place_ref[4]
    rows = out_refs[0].shape[1]
    a_own = token_rows(a_ref, core)
    a_other = token_rows(a_ref, 1 - core)
    half = a_own.shape[1] // 2
    for ky in range(side):
        for kz in range(side):
            row = lax.rem(y + ky, side) * side + lax.rem(z + kz, side)
            start = pl.multiple_of(row * rows, rows)
            part = mm(own_ref[:, pl.ds(start, rows)], a_own, TN) + mm(other_ref[:, pl.ds(start, rows)], a_other, TN)
            out_refs[kz][ky] = part[:, :half].astype(BF16)
            out_refs[side + ky][kz] = part[:, half:].astype(BF16)


def grad_weight_parts(place, own, other, a, side):
    tokens, features = own.shape
    columns = a.shape[0] * a.shape[1] * a.shape[3]
    rows = features // side**2
    return pl.pallas_call(
        functools.partial(grad_weight_kernel, side),
        out_shape=(jax.ShapeDtypeStruct((side, rows, columns // 2), BF16),) * (2 * side),
        in_specs=[SMEM] + [VMEM] * 3,
        out_specs=(VMEM,) * (2 * side),
        compiler_params=pltpu.CompilerParams(vmem_limit_bytes=32 * MIB),
        cost_estimate=cost(4 * tokens * features * columns, 7 * MIB),
        name="grad_weight_parts",
    )(place, own, other, a)


def summed(parts):
    total = parts[0].astype(F32)
    for part in parts[1:]:
        total = total + part.astype(F32)
    return total


def per_device(queries, key_states, value_states, grad_output, out_weight, key_tiles, tile_count):
    seq = lax.axis_size("seq")
    ranks = lax.axis_size("dp")
    side = math.isqrt(ranks)
    chips = seq // 2
    s_index = lax.axis_index("seq")
    d_index = lax.axis_index("dp")
    core = lax.rem(s_index, 2)
    tokens, columns = queries.shape[1:]
    heads, units, width = key_tiles.shape[1:]
    head_dim = columns // heads
    rows = out_weight.shape[0]
    place = jnp.stack([s_index, jnp.int32(seq), core, lax.div(d_index, side), lax.rem(d_index, side)]).astype(jnp.int32)
    lists = key_tiles.reshape(-1)
    counts = tile_count.reshape(-1)
    same_core = [list(range(c, seq, 2)) for c in range(2)]
    across = [(i, i ^ 1) for i in range(seq)]

    def y_shift(k):
        return [(i, (i // side + k) % side * side + i % side) for i in range(ranks)]

    def z_shift(k):
        return [(i, i // side * side + (i % side + k) % side) for i in range(ranks)]

    def x_swap(k):
        return [(i, i ^ (2 * k)) for i in range(seq)]

    def over_chips(values):
        return lax.all_to_all(values, "seq", split_axis=0, concat_axis=0, tiled=True, axis_index_groups=same_core)

    by_core = out_weight.reshape(rows, 2, chips, 2, head_dim)
    half_shard = lax.dynamic_index_in_dim(by_core, core, axis=3, keepdims=False)
    half_shard = half_shard.transpose(0, 2, 1, 3).reshape(rows, columns // 2)
    weights = lax.all_gather(half_shard, "dp", axis=0, tiled=True)

    qkv = lax.all_to_all(pack(queries, key_states, value_states, seq, head_dim), "seq", split_axis=0, concat_axis=0, tiled=True)
    own_rows = grad_output[0]
    other_rows = lax.ppermute(own_rows, "seq", across)
    g = over_chips(grad_attn(place, own_rows, other_rows, weights, chips))
    a, lse = attention_forward(place, lists, counts, qkv, chips, width)
    a_home = over_chips(a)
    grads = attention_backward(place, lists, counts, qkv, g, a, lse, width)
    parts = grad_weight_parts(place, own_rows, other_rows, a_home, side)
    grads_home = lax.all_to_all(grads, "seq", split_axis=0, concat_axis=0, tiled=True)

    z_first = [parts[0]] + [lax.ppermute(parts[k], "dp", z_shift(k)) for k in range(1, side)]
    y_first = [parts[side]] + [lax.ppermute(parts[side + k], "dp", y_shift(k)) for k in range(1, side)]
    out_own, out_other = project(place, a_home, weights)
    output = (out_own + lax.ppermute(out_other, "seq", across).astype(F32)).astype(BF16)
    z_sum = summed(z_first).astype(BF16)
    y_sum = summed(y_first).astype(BF16)
    z_done = summed([z_sum[0]] + [lax.ppermute(z_sum[k], "dp", y_shift(k)) for k in range(1, side)])
    y_done = summed([y_sum[0]] + [lax.ppermute(y_sum[k], "dp", z_shift(k)) for k in range(1, side)])
    chip_share = jnp.concatenate([z_done, y_done], axis=1).astype(BF16)
    by_chip = [chip_share] + [lax.ppermute(chip_share, "seq", x_swap(k)) for k in range(1, chips)]
    while len(by_chip) > 1:
        by_chip = [summed(by_chip[i : i + 2]) for i in range(0, len(by_chip), 2)]
    own_half = by_chip[0].astype(BF16)
    other_half = lax.ppermute(own_half, "seq", across)
    even = jnp.where(core == 0, own_half, other_half).reshape(rows, chips, 2, head_dim)
    odd = jnp.where(core == 0, other_half, own_half).reshape(rows, chips, 2, head_dim)
    grad_weight = jnp.stack([even, odd], axis=2).transpose(0, 3, 1, 2, 4).reshape(rows, columns).astype(F32)

    grad_query, grad_key, grad_value = unpack(grads_home)
    return output[None], grad_query, grad_key, grad_value, grad_weight


def solution(mesh):
    in_specs = (
        P("dp", "seq", None),
        P("dp", "seq", None),
        P("dp", "seq", None),
        P("dp", "seq", None),
        P("dp", None),
        P("dp", None, None, None),
        P("dp", None, None),
    )
    out_specs = (
        P("dp", "seq", None),
        P("dp", "seq", None),
        P("dp", "seq", None),
        P("dp", "seq", None),
        P("dp", None),
    )
    return jax.shard_map(per_device, mesh=mesh, in_specs=in_specs, out_specs=out_specs, check_vma=False)
```

```python
import functools
import math

import jax
import jax.numpy as jnp
from jax import lax
from jax.experimental import pallas as pl
from jax.experimental.pallas import tpu as pltpu
from jax.sharding import PartitionSpec as P

NN = (((1,), (0,)), ((), ()))
NT = (((1,), (1,)), ((), ()))
TN = (((0,), (0,)), ((), ()))
F32 = jnp.float32
BF16 = jnp.bfloat16
MIB = 2**20
SMEM = pl.BlockSpec(memory_space=pltpu.SMEM)
VMEM = pl.BlockSpec(memory_space=pltpu.VMEM)
ANY = pl.BlockSpec(memory_space=pl.ANY)
HBM = pl.BlockSpec(memory_space=pltpu.HBM)
TILE = 128
UNITS_AT_ONCE = 4
VMEM_LIMIT = 60 * MIB


def mm(a, b, dims=NN):
    return lax.dot_general(a, b, dims, preferred_element_type=F32)


def cost(flops, moved, exps=0):
    return pl.CostEstimate(flops=flops, bytes_accessed=moved, transcendentals=exps)


def pack_kernel(q_ref, k_ref, v_ref, out_ref):
    seq, _, halves, _, width = out_ref.shape
    for n, ref in enumerate((q_ref, k_ref, v_ref)):
        for s in range(seq):
            for half in range(halves):
                column = (s + seq * half) * width
                out_ref[s, n, half] = ref[0, :, column : column + width]


def pack(q, k, v, seq, head_dim):
    _, tokens, columns = q.shape
    halves = columns // (seq * head_dim)
    rows = tokens // 4
    return pl.pallas_call(
        pack_kernel,
        grid=(tokens // rows,),
        out_shape=jax.ShapeDtypeStruct((seq, 3, halves, tokens, head_dim), q.dtype),
        in_specs=[pl.BlockSpec((1, rows, columns), lambda i: (0, i, 0))] * 3,
        out_specs=pl.BlockSpec((seq, 3, halves, rows, head_dim), lambda i: (0, 0, 0, i, 0)),
        compiler_params=pltpu.CompilerParams(vmem_limit_bytes=VMEM_LIMIT),
        cost_estimate=cost(0, 12 * tokens * columns),
        name="pack_heads",
    )(q, k, v)


def unpack_kernel(in_ref, q_ref, k_ref, v_ref):
    seq, _, halves, _, width = in_ref.shape
    for n, ref in enumerate((q_ref, k_ref, v_ref)):
        for s in range(seq):
            for half in range(halves):
                column = (s + seq * half) * width
                ref[0, :, column : column + width] = in_ref[s, n, half]


def unpack(blocks):
    seq, _, halves, tokens, head_dim = blocks.shape
    columns = seq * halves * head_dim
    rows = tokens // 4
    return pl.pallas_call(
        unpack_kernel,
        grid=(tokens // rows,),
        out_shape=(jax.ShapeDtypeStruct((1, tokens, columns), blocks.dtype),) * 3,
        in_specs=[pl.BlockSpec((seq, 3, halves, rows, head_dim), lambda i: (0, 0, 0, i, 0))],
        out_specs=(pl.BlockSpec((1, rows, columns), lambda i: (0, i, 0)),) * 3,
        compiler_params=pltpu.CompilerParams(vmem_limit_bytes=VMEM_LIMIT),
        cost_estimate=cost(0, 12 * tokens * columns),
        name="unpack_heads",
    )(blocks)


def core_columns(core, chips):
    return [pl.multiple_of((2 * x + core + 2 * chips * half) * TILE, TILE) for x in range(chips) for half in range(2)]


def pack_weight_kernel(chips, place_ref, in_ref, after_ref, out_ref):
    for i, column in enumerate(core_columns(place_ref[2], chips)):
        out_ref[:, pl.ds(i * TILE, TILE)] = in_ref[:, pl.ds(column, TILE)]


def pack_weight(place, shard, after, chips):
    rows, columns = shard.shape
    return pl.pallas_call(
        functools.partial(pack_weight_kernel, chips),
        out_shape=jax.ShapeDtypeStruct((rows, columns // 2), shard.dtype),
        in_specs=[SMEM, VMEM, HBM],
        out_specs=VMEM,
        compiler_params=pltpu.CompilerParams(vmem_limit_bytes=VMEM_LIMIT),
        cost_estimate=cost(0, 3 * rows * columns),
        name="pack_weight",
    )(place, shard, after)


def unpack_weight_kernel(chips, place_ref, own_ref, other_ref, out_ref):
    for ref, core in ((own_ref, place_ref[2]), (other_ref, 1 - place_ref[2])):
        for i, column in enumerate(core_columns(core, chips)):
            out_ref[:, pl.ds(column, TILE)] = ref[:, pl.ds(i * TILE, TILE)].astype(F32)


def unpack_weight(place, own, other, chips):
    rows, columns = own.shape
    return pl.pallas_call(
        functools.partial(unpack_weight_kernel, chips),
        out_shape=jax.ShapeDtypeStruct((rows, 2 * columns), F32),
        in_specs=[SMEM, VMEM, VMEM],
        out_specs=VMEM,
        compiler_params=pltpu.CompilerParams(vmem_limit_bytes=VMEM_LIMIT),
        cost_estimate=cost(0, 12 * rows * columns),
        name="unpack_weight",
    )(place, own, other)


def slot_plan(place_ref, tiles_ref, counts_ref, unit, slot, units, width):
    first_head = place_ref[0]
    split = counts_ref[first_head * units + unit]
    in_first = slot < split
    head = jnp.where(in_first, first_head, first_head + place_ref[1])
    entry = jnp.minimum(jnp.where(in_first, slot, width - slot), width - 1)
    tile = tiles_ref[(head * units + unit) * width + entry]
    return in_first, jnp.where(in_first, 0, 1), tile


def rows_of(ref, half, tile):
    per_block = ref.shape[2] // TILE
    start = pl.multiple_of(lax.rem(tile, per_block) * TILE, TILE)
    return ref.at[lax.div(tile, per_block), half, pl.ds(start, TILE), :]


def forward_kernel(multi, slots, units, width, scale, place_ref, tiles_ref, counts_ref, qkv_ref, a_ref, lse_ref, *refs):
    block_refs, (vt_ref, s_ref, p_ref) = refs[:-3], refs[-3:]
    scale2 = scale * math.log2(math.e)
    q_ref, k_ref, v_ref = (qkv_ref.at[:, n] for n in range(3))

    @pl.loop(0, units, unroll=2)
    def _(t):
        for half in range(2):
            vt_ref[half * units + t] = rows_of(v_ref, half, t)[...].T

    @pl.loop(0, units // multi)
    def _(step):
        plans = [[slot_plan(place_ref, tiles_ref, counts_ref, step * multi + u, j, units, width) for j in range(slots)] for u in range(multi)]
        all_tops = []
        for u in range(multi):
            tops = []
            for j, (in_first, half, tile) in enumerate(plans[u]):
                s = mm(rows_of(k_ref, half, tile)[...], rows_of(q_ref, half, step * multi + u)[...], NT)
                s_ref[u * slots + j] = s
                tops.append(jnp.max(s.reshape(TILE // 8, 8, TILE), axis=0))
            all_tops.append(tops)
        low = jnp.full((8, TILE), -jnp.inf, F32)
        zero = jnp.zeros((TILE, TILE), BF16)
        stats = []
        for u in range(multi):
            top = []
            for half in range(2):
                m = low
                for (in_first, _, _), t8 in zip(plans[u], all_tops[u]):
                    use = in_first if half == 0 else jnp.logical_not(in_first)
                    m = jnp.maximum(m, jnp.where(use, t8, low))
                top.append(jnp.max(m, axis=0, keepdims=True) * scale2)
            totals = [jnp.zeros((8, TILE), F32)] * 2
            for j, (in_first, half, tile) in enumerate(plans[u]):
                p = jnp.exp2(s_ref[u * slots + j] * scale2 - jnp.where(in_first, top[0], top[1]))
                l8 = jnp.sum(p.reshape(TILE // 8, 8, TILE), axis=0)
                totals[0] = totals[0] + jnp.where(in_first, l8, 0.0)
                totals[1] = totals[1] + jnp.where(in_first, 0.0, l8)
                pb = p.astype(BF16)
                p_ref[u, pl.ds(j * TILE, TILE), 0:TILE] = jnp.where(in_first, pb, zero)
                p_ref[u, pl.ds(j * TILE, TILE), TILE : 2 * TILE] = jnp.where(in_first, zero, pb)
            stats.append((top, totals))
        for u in range(multi):
            unit = step * multi + u
            top, totals = stats[u]
            vt = jnp.concatenate([vt_ref[half * units + tile] for _, half, tile in plans[u]], axis=1)
            mixed = mm(vt, p_ref[u])
            for half in range(2):
                total = jnp.sum(totals[half], axis=0, keepdims=True)
                a_t = mixed[:, half * TILE : (half + 1) * TILE] / total
                rows_of(a_ref, half, unit)[...] = a_t.T.astype(BF16)
                lse_ref[half * units + unit] = jnp.broadcast_to(top[half] + jnp.log2(total), (8, TILE))

    chips = len(block_refs)
    for k, ref in enumerate(block_refs):
        ref[...] = a_ref[lax.rem(place_ref[5] + k, chips)]


def attention_forward(place, tiles, counts, qkv, chips, width):
    seq, _, halves, tokens, head_dim = qkv.shape
    units = seq * tokens // TILE
    slots = width + 1
    rows = seq * tokens // chips
    return pl.pallas_call(
        functools.partial(forward_kernel, UNITS_AT_ONCE, slots, units, width, 1.0 / math.sqrt(head_dim)),
        out_shape=(
            jax.ShapeDtypeStruct((chips, halves, rows, head_dim), BF16),
            jax.ShapeDtypeStruct((halves * units, 8, TILE), F32),
        )
        + (jax.ShapeDtypeStruct((halves, rows, head_dim), BF16),) * chips,
        in_specs=[SMEM] * 3 + [VMEM],
        out_specs=(VMEM,) * (2 + chips),
        scratch_shapes=[
            pltpu.VMEM((halves * units, head_dim, TILE), BF16),
            pltpu.VMEM((UNITS_AT_ONCE * slots, TILE, TILE), F32),
            pltpu.VMEM((UNITS_AT_ONCE, slots * TILE, 2 * TILE), BF16),
        ],
        compiler_params=pltpu.CompilerParams(vmem_limit_bytes=VMEM_LIMIT),
        cost_estimate=cost(16 * units * slots * TILE**3, 6 * MIB, units * slots * TILE * TILE),
        name="attention_forward",
    )(place, tiles, counts, qkv)


def backward_kernel(multi, slots, units, width, scale, place_ref, tiles_ref, counts_ref, qkv_ref, g_ref, a_ref, lse_ref, *refs):
    out_ref, kt_ref, dk_acc, dv_acc, s_ref, dp_ref, p_ref, d_ref = refs[-8:]
    scale2 = scale * math.log2(math.e)
    q_ref, k_ref, v_ref = (qkv_ref.at[:, n] for n in range(3))
    dq_ref, dk_ref, dv_ref = (out_ref.at[:, n] for n in range(3))

    @pl.loop(0, units, unroll=2)
    def _(t):
        for half in range(2):
            kt_ref[half * units + t] = rows_of(k_ref, half, t)[...].T
            dk_acc[half * units + t] = jnp.zeros((TILE, TILE), F32)
            dv_acc[half * units + t] = jnp.zeros((TILE, TILE), F32)

    @pl.loop(0, units // multi)
    def _(step):
        plans = [[slot_plan(place_ref, tiles_ref, counts_ref, step * multi + u, j, units, width) for j in range(slots)] for u in range(multi)]
        zero = jnp.zeros((TILE, TILE), BF16)
        deltas, lses = [], []
        for u in range(multi):
            unit = step * multi + u
            delta, lse = [], []
            for half in range(2):
                prod = rows_of(g_ref, half, unit)[...].astype(F32) * rows_of(a_ref, half, unit)[...].astype(F32)
                delta.append(jnp.sum(prod.T, axis=0, keepdims=True))
                lse.append(lse_ref[half * units + unit][0:1])
            deltas.append(delta)
            lses.append(lse)
            for j, (in_first, half, tile) in enumerate(plans[u]):
                s_ref[u * slots + j] = mm(rows_of(k_ref, half, tile)[...], rows_of(q_ref, half, unit)[...], NT)
                dp_ref[u * slots + j] = mm(rows_of(v_ref, half, tile)[...], rows_of(g_ref, half, unit)[...], NT)
        for u in range(multi):
            for j, (in_first, half, tile) in enumerate(plans[u]):
                p = jnp.exp2(s_ref[u * slots + j] * scale2 - jnp.where(in_first, lses[u][0], lses[u][1]))
                ds = (p * (dp_ref[u * slots + j] - jnp.where(in_first, deltas[u][0], deltas[u][1]))).astype(BF16)
                p_ref[u * slots + j] = p.astype(BF16)
                d_ref[u, pl.ds(j * TILE, TILE), 0:TILE] = jnp.where(in_first, ds, zero)
                d_ref[u, pl.ds(j * TILE, TILE), TILE : 2 * TILE] = jnp.where(in_first, zero, ds)
        for u in range(multi):
            unit = step * multi + u
            for j, (in_first, half, tile) in enumerate(plans[u]):
                ds = d_ref[u, pl.ds(j * TILE, TILE), pl.ds(pl.multiple_of(half * TILE, TILE), TILE)]
                dv_acc[half * units + tile] += mm(p_ref[u * slots + j], rows_of(g_ref, half, unit)[...])
                dk_acc[half * units + tile] += mm(ds, rows_of(q_ref, half, unit)[...])
            kt = jnp.concatenate([kt_ref[half * units + tile] for _, half, tile in plans[u]], axis=1)
            dq_t = mm(kt, d_ref[u]) * scale
            for half in range(2):
                rows_of(dq_ref, half, unit)[...] = dq_t[:, half * TILE : (half + 1) * TILE].T.astype(BF16)

    @pl.loop(0, units, unroll=2)
    def _(t):
        for half in range(2):
            rows_of(dk_ref, half, t)[...] = (dk_acc[half * units + t] * scale).astype(BF16)
            rows_of(dv_ref, half, t)[...] = dv_acc[half * units + t].astype(BF16)


def attention_backward(place, tiles, counts, qkv, g, a, lse, after, width):
    seq, _, halves, tokens, head_dim = qkv.shape
    units = seq * tokens // TILE
    slots = width + 1
    return pl.pallas_call(
        functools.partial(backward_kernel, UNITS_AT_ONCE, slots, units, width, 1.0 / math.sqrt(head_dim)),
        out_shape=jax.ShapeDtypeStruct(qkv.shape, BF16),
        in_specs=[SMEM] * 3 + [VMEM] * 4 + [HBM] * len(after),
        out_specs=VMEM,
        scratch_shapes=[
            pltpu.VMEM((halves * units, head_dim, TILE), BF16),
            pltpu.VMEM((halves * units, TILE, head_dim), F32),
            pltpu.VMEM((halves * units, TILE, head_dim), F32),
            pltpu.VMEM((UNITS_AT_ONCE * slots, TILE, TILE), F32),
            pltpu.VMEM((UNITS_AT_ONCE * slots, TILE, TILE), F32),
            pltpu.VMEM((UNITS_AT_ONCE * slots, TILE, TILE), BF16),
            pltpu.VMEM((UNITS_AT_ONCE, slots * TILE, 2 * TILE), BF16),
        ],
        compiler_params=pltpu.CompilerParams(vmem_limit_bytes=VMEM_LIMIT),
        cost_estimate=cost(3*10**11, MIB),
        name="attention_backward",
    )(place, tiles, counts, qkv, g, a, lse, *after)


def grad_attn_kernel(place_ref, own_ref, other_ref, w_ref, after_ref, g_ref):
    tokens = own_ref.shape[0]
    core = place_ref[2]
    rows = jnp.concatenate([own_ref[...], other_ref[...]], axis=0)
    g = mm(rows, w_ref[...]).astype(BF16)
    for slot, first in ((core, 0), (1 - core, tokens)):
        target = pl.ds(pl.multiple_of(slot * tokens, tokens), tokens)
        for half in range(2):
            g_ref[0, half, target, :] = g[first : first + tokens, half * TILE : (half + 1) * TILE]


def grad_attn(place, own, other, weights, after, chips):
    tokens, depth = own.shape
    columns = weights.shape[1]
    block = columns // chips
    return pl.pallas_call(
        grad_attn_kernel,
        grid=(chips,),
        out_shape=jax.ShapeDtypeStruct((chips, 2, 2 * tokens, TILE), BF16),
        in_specs=[
            SMEM,
            pl.BlockSpec((tokens, depth), lambda i: (0, 0)),
            pl.BlockSpec((tokens, depth), lambda i: (0, 0)),
            pl.BlockSpec((depth, block), lambda i: (0, i)),
            HBM,
        ],
        out_specs=pl.BlockSpec((1, 2, 2 * tokens, TILE), lambda i: (i, 0, 0, 0)),
        compiler_params=pltpu.CompilerParams(vmem_limit_bytes=VMEM_LIMIT),
        cost_estimate=cost(4 * tokens * depth * columns, 7 * MIB),
        name="grad_attn",
    )(place, own, other, weights, after)


def gather_rows(place_ref, block_refs, rows_ref):
    chips = len(block_refs)
    halves, rows, width = block_refs[0].shape
    tokens = rows // 2
    core = place_ref[2]
    for k, ref in enumerate(block_refs):
        chip = lax.rem(place_ref[5] + chips - k, chips)
        for half in range(halves):
            target = pl.ds(pl.multiple_of((chip * halves + half) * width, width), width)
            for slot, first in ((core, 0), (1 - core, tokens)):
                source = pl.ds(pl.multiple_of(slot * tokens, tokens), tokens)
                rows_ref[first : first + tokens, target] = ref[half, source, :]


def project_kernel(place_ref, *refs):
    block_refs, w_ref, own_ref, other_ref, rows_ref = refs[:-5], refs[-5], refs[-3], refs[-2], refs[-1]

    @pl.when(pl.program_id(0) == 0)
    def _():
        gather_rows(place_ref, block_refs, rows_ref)

    tokens = own_ref.shape[0]
    out = mm(rows_ref[...], w_ref[...], NT)
    own_ref[...] = out[:tokens]
    other_ref[...] = out[tokens:].astype(BF16)


def project(place, blocks, weights, after):
    features, columns = weights.shape
    tokens = blocks[0].shape[1] // 2
    step = 2 * TILE
    return pl.pallas_call(
        project_kernel,
        grid=(features // step,),
        out_shape=(jax.ShapeDtypeStruct((tokens, features), F32), jax.ShapeDtypeStruct((tokens, features), BF16)),
        in_specs=[SMEM]
        + [pl.BlockSpec(block.shape, lambda i: (0, 0, 0)) for block in blocks]
        + [pl.BlockSpec((step, columns), lambda i: (i, 0)), HBM],
        out_specs=(pl.BlockSpec((tokens, step), lambda i: (0, i)),) * 2,
        scratch_shapes=[pltpu.VMEM((2 * tokens, columns), BF16)],
        compiler_params=pltpu.CompilerParams(vmem_limit_bytes=VMEM_LIMIT),
        cost_estimate=cost(4 * tokens * features * columns, 8 * MIB),
        name="project",
    )(place, *blocks, weights, after)


def grad_weight_kernel(side, chips, place_ref, own_ref, other_ref, *refs):
    block_refs, out_refs, (rows_ref, part_ref, sems) = refs[:chips], refs[chips:-3], refs[-3:]
    gather_rows(place_ref, block_refs, rows_ref)
    rows = part_ref.shape[2]
    half = part_ref.shape[3]
    copies = [pltpu.make_async_copy(part_ref.at[n], out_refs[n], sems.at[n]) for n in range(2 * side)]
    for ky in range(side):
        for kz in range(side):
            row = lax.rem(place_ref[3] + ky, side) * side + lax.rem(place_ref[4] + kz, side)
            columns = pl.ds(pl.multiple_of(row * rows, rows), rows)
            left = jnp.concatenate([own_ref[:, columns], other_ref[:, columns]], axis=0)
            part = mm(left, rows_ref[...], TN)
            part_ref[kz, ky] = part[:, :half].astype(BF16)
            part_ref[side + ky, kz] = part[:, half:].astype(BF16)
            if ky == side - 1:
                copies[kz].start()
        copies[side + ky].start()
    for copy in copies:
        copy.wait()


def grad_weight_parts(place, own, other, blocks, side):
    tokens, features = own.shape
    chips = len(blocks)
    columns = chips * blocks[0].shape[0] * blocks[0].shape[2]
    rows = features // side**2
    return pl.pallas_call(
        functools.partial(grad_weight_kernel, side, chips),
        out_shape=(jax.ShapeDtypeStruct((side, rows, columns // 2), BF16),) * (2 * side),
        in_specs=[SMEM] + [VMEM] * (2 + chips),
        out_specs=(HBM,) * (2 * side),
        scratch_shapes=[
            pltpu.VMEM((2 * tokens, columns), BF16),
            pltpu.VMEM((2 * side, side, rows, columns // 2), BF16),
            pltpu.SemaphoreType.DMA((2 * side,)),
        ],
        compiler_params=pltpu.CompilerParams(vmem_limit_bytes=VMEM_LIMIT),
        cost_estimate=cost(4 * tokens * features * columns, 7 * MIB),
        name="grad_weight_parts",
    )(place, own, other, *blocks)


def gate_kernel(*refs):
    del refs


def gate(values, *after):
    return pl.pallas_call(
        gate_kernel,
        out_shape=jax.ShapeDtypeStruct(values.shape, values.dtype),
        in_specs=[ANY] * (1 + len(after)),
        out_specs=ANY,
        input_output_aliases={0: 0},
        compiler_params=pltpu.CompilerParams(vmem_limit_bytes=VMEM_LIMIT),
        name="gate",
    )(values, *after)


def sum_kernel(*refs):
    side = len(refs) // 4
    for n in range(2):
        in_refs = refs[n * side : (n + 1) * side]
        for k in range(side):
            total = in_refs[0][k].astype(F32)
            for ref in in_refs[1:]:
                total = total + ref[k].astype(F32)
            refs[2 * side + n * side + k][...] = total.astype(BF16)


def summed(first, second):
    side, rows, width = first[0].shape
    sums = pl.pallas_call(
        sum_kernel,
        out_shape=(jax.ShapeDtypeStruct((rows, width), BF16),) * (2 * side),
        in_specs=[VMEM] * (2 * side),
        out_specs=(VMEM,) * (2 * side),
        compiler_params=pltpu.CompilerParams(vmem_limit_bytes=VMEM_LIMIT),
        cost_estimate=cost(10**12, MIB),
        name="summed",
    )(*first, *second)
    return sums[:side], sums[side:]


def sum_pair_kernel(*refs):
    out_ref = refs[-1]
    count = len(refs) // 2
    width = refs[0].shape[1]
    for side in range(2):
        total = refs[side * count][...].astype(F32)
        for ref in refs[side * count + 1 : (side + 1) * count]:
            total = total + ref[...].astype(F32)
        out_ref[:, side * width : (side + 1) * width] = total.astype(BF16)


def summed_side_by_side(first, second):
    rows, width = first[0].shape
    return pl.pallas_call(
        sum_pair_kernel,
        out_shape=jax.ShapeDtypeStruct((rows, 2 * width), BF16),
        in_specs=[VMEM] * (2 * len(first)),
        out_specs=VMEM,
        compiler_params=pltpu.CompilerParams(vmem_limit_bytes=VMEM_LIMIT),
        cost_estimate=cost(0, 4 * (len(first) + 1) * rows * width),
        name="summed_side_by_side",
    )(*first, *second)


def sum_chips_kernel(a_ref, b_ref, c_ref, d_ref, *refs):
    first = a_ref[...].astype(F32) + b_ref[...].astype(F32)
    second = c_ref[...].astype(F32) + d_ref[...].astype(F32)
    refs[-1][...] = (first + second).astype(BF16)


def summed_over_chips(parts, after):
    return pl.pallas_call(
        sum_chips_kernel,
        out_shape=jax.ShapeDtypeStruct(parts[0].shape, BF16),
        in_specs=[VMEM] * len(parts) + [HBM] * len(after),
        out_specs=VMEM,
        compiler_params=pltpu.CompilerParams(vmem_limit_bytes=VMEM_LIMIT),
        cost_estimate=cost(0, 10 * math.prod(parts[0].shape)),
        name="summed_over_chips",
    )(*parts, *after)


def per_device(queries, key_states, value_states, grad_output, out_weight, key_tiles, tile_count):
    seq = lax.axis_size("seq")
    ranks = lax.axis_size("dp")
    side = math.isqrt(ranks)
    chips = seq // 2
    s_index = lax.axis_index("seq")
    d_index = lax.axis_index("dp")
    core = lax.rem(s_index, 2)
    tokens, columns = queries.shape[1:]
    heads, units, width = key_tiles.shape[1:]
    head_dim = columns // heads
    rows = out_weight.shape[0]
    place = jnp.stack([s_index, jnp.int32(seq), core, lax.div(d_index, side), lax.rem(d_index, side), lax.div(s_index, 2)]).astype(jnp.int32)
    lists = key_tiles.reshape(-1)
    counts = tile_count.reshape(-1)
    same_core = [list(range(c, seq, 2)) for c in range(2)]
    across = [(i, i ^ 1) for i in range(seq)]

    def y_shift(k):
        return [(i, (i // side + k) % side * side + i % side) for i in range(ranks)]

    def z_shift(k):
        return [(i, i // side * side + (i % side + k) % side) for i in range(ranks)]

    def x_shift(k):
        return [(i, (i + 2 * k) % seq) for i in range(seq)]

    def x_swap(k):
        return [(i, i ^ (2 * k)) for i in range(seq)]

    def over_chips(values):
        return lax.all_to_all(values, "seq", split_axis=0, concat_axis=0, tiled=True, axis_index_groups=same_core)

    packed = pack(queries, key_states, value_states, seq, head_dim)
    weights = lax.all_gather(pack_weight(place, out_weight, packed, chips), "dp", axis=0, tiled=True)
    qkv = lax.all_to_all(packed, "seq", split_axis=0, concat_axis=0, tiled=True)
    own_rows = grad_output[0]
    other_rows = lax.ppermute(own_rows, "seq", across)
    a, lse, *a_blocks = attention_forward(place, lists, counts, qkv, chips, width)
    a_home = [a_blocks[0]] + [lax.ppermute(a_blocks[k], "seq", x_shift(k)) for k in range(1, chips)]
    g = over_chips(gate(grad_attn(place, own_rows, other_rows, weights, lse, chips), *a_home))
    parts = grad_weight_parts(place, own_rows, other_rows, a_home, side)
    z_first = [parts[0]] + [lax.ppermute(parts[k], "dp", z_shift(k)) for k in range(1, side)]
    y_first = [parts[side]] + [lax.ppermute(parts[side + k], "dp", y_shift(k)) for k in (1, side - 1)]
    grads = attention_backward(place, lists, counts, qkv, g, a, lse, (parts[0],), width)
    grads_home = lax.all_to_all(grads, "seq", split_axis=0, concat_axis=0, tiled=True)
    y_first += [lax.ppermute(gate(parts[side + k], grads), "dp", y_shift(k)) for k in range(2, side - 1)]

    z_sum, y_sum = summed(z_first, y_first)
    out_own, out_other = project(place, a_home, weights, grads)
    output = (out_own + lax.ppermute(out_other, "seq", across).astype(F32)).astype(BF16)
    chip_share = summed_side_by_side(
        [z_sum[0]] + [lax.ppermute(z_sum[k], "dp", y_shift(k)) for k in range(1, side)],
        [y_sum[0]] + [lax.ppermute(y_sum[k], "dp", z_shift(k)) for k in range(1, side)],
    )
    grad_query, grad_key, grad_value = unpack(grads_home)
    by_chip = [chip_share] + [lax.ppermute(chip_share, "seq", x_swap(k)) for k in range(1, chips)]
    own_half = summed_over_chips(by_chip, (grad_query, output))
    grad_weight = unpack_weight(place, own_half, lax.ppermute(own_half, "seq", across), chips)
    return output[None], grad_query, grad_key, grad_value, grad_weight


def solution(mesh):
    in_specs = (
        P("dp", "seq", None),
        P("dp", "seq", None),
        P("dp", "seq", None),
        P("dp", "seq", None),
        P("dp", None),
        P("dp", None, None, None),
        P("dp", None, None),
    )
    out_specs = (
        P("dp", "seq", None),
        P("dp", "seq", None),
        P("dp", "seq", None),
        P("dp", "seq", None),
        P("dp", None),
    )
    return jax.shard_map(per_device, mesh=mesh, in_specs=in_specs, out_specs=out_specs, check_vma=False)
```

```python
import functools
import math

import jax
import jax.numpy as jnp
from jax import lax
from jax.experimental import pallas as pl
from jax.experimental.pallas import tpu as pltpu
from jax.sharding import PartitionSpec as P

NN = (((1,), (0,)), ((), ()))
NT = (((1,), (1,)), ((), ()))
TN = (((0,), (0,)), ((), ()))
F32 = jnp.float32
BF16 = jnp.bfloat16
MIB = 2**20
SMEM = pl.BlockSpec(memory_space=pltpu.SMEM)
VMEM = pl.BlockSpec(memory_space=pltpu.VMEM)
ANY = pl.BlockSpec(memory_space=pl.ANY)
HBM = pl.BlockSpec(memory_space=pltpu.HBM)
TILE = 128
UNITS_AT_ONCE = 4
VMEM_LIMIT = 60 * MIB


def mm(a, b, dims=NN):
    return lax.dot_general(a, b, dims, preferred_element_type=F32)


def cost(flops, moved, exps=0):
    return pl.CostEstimate(flops=flops, bytes_accessed=moved, transcendentals=exps)


def pack_kernel(q_ref, k_ref, v_ref, out_ref, rows_ref, in_sems, out_sems):
    seq, _, halves, _, width = out_ref.shape
    loads = [pltpu.make_async_copy(ref.at[0], rows_ref.at[n], in_sems.at[n]) for n, ref in enumerate((q_ref, k_ref, v_ref))]
    for load in loads:
        load.start()
    stores = []
    for n, load in enumerate(loads):
        load.wait()
        for s in range(seq):
            for half in range(halves):
                source = rows_ref.at[n, :, pl.ds((s + seq * half) * width, width)]
                stores.append(pltpu.make_async_copy(source, out_ref.at[s, n, half], out_sems.at[len(stores)]))
                stores[-1].start()
    for store in stores:
        store.wait()


def pack(q, k, v, seq, head_dim):
    _, tokens, columns = q.shape
    halves = columns // (seq * head_dim)
    return pl.pallas_call(
        pack_kernel,
        out_shape=jax.ShapeDtypeStruct((seq, 3, halves, tokens, head_dim), q.dtype),
        in_specs=[HBM] * 3,
        out_specs=HBM,
        scratch_shapes=[
            pltpu.VMEM((3, tokens, columns), q.dtype),
            pltpu.SemaphoreType.DMA((3,)),
            pltpu.SemaphoreType.DMA((3 * seq * halves,)),
        ],
        compiler_params=pltpu.CompilerParams(vmem_limit_bytes=VMEM_LIMIT),
        cost_estimate=cost(0, 12 * tokens * columns),
        name="pack_heads",
    )(q, k, v)


def unpack_kernel(in_ref, q_ref, k_ref, v_ref):
    seq, _, halves, _, width = in_ref.shape
    for n, ref in enumerate((q_ref, k_ref, v_ref)):
        for s in range(seq):
            for half in range(halves):
                column = (s + seq * half) * width
                ref[0, :, column : column + width] = in_ref[s, n, half]


def unpack(blocks):
    seq, _, halves, tokens, head_dim = blocks.shape
    columns = seq * halves * head_dim
    rows = tokens // 4
    return pl.pallas_call(
        unpack_kernel,
        grid=(tokens // rows,),
        out_shape=(jax.ShapeDtypeStruct((1, tokens, columns), blocks.dtype),) * 3,
        in_specs=[pl.BlockSpec((seq, 3, halves, rows, head_dim), lambda i: (0, 0, 0, i, 0))],
        out_specs=(pl.BlockSpec((1, rows, columns), lambda i: (0, i, 0)),) * 3,
        compiler_params=pltpu.CompilerParams(vmem_limit_bytes=VMEM_LIMIT),
        cost_estimate=cost(0, 12 * tokens * columns),
        name="unpack_heads",
    )(blocks)


def core_columns(core, chips):
    return [pl.multiple_of((2 * x + core + 2 * chips * half) * TILE, TILE) for x in range(chips) for half in range(2)]


def pack_weight_kernel(chips, place_ref, in_ref, *out_refs):
    for i, column in enumerate(core_columns(place_ref[2], chips)):
        out_refs[i // chips][:, pl.ds(i % chips * TILE, TILE)] = in_ref[:, pl.ds(column, TILE)]


def pack_weight(place, shard, chips):
    rows, columns = shard.shape
    return pl.pallas_call(
        functools.partial(pack_weight_kernel, chips),
        out_shape=(jax.ShapeDtypeStruct((rows, columns // 4), shard.dtype),) * 2,
        in_specs=[SMEM, VMEM],
        out_specs=(VMEM,) * 2,
        compiler_params=pltpu.CompilerParams(vmem_limit_bytes=VMEM_LIMIT),
        cost_estimate=cost(0, 3 * rows * columns),
        name="pack_weight",
    )(place, shard)


def stack_kernel(*refs):
    count = len(refs) // 2 - 1
    for n in range(2):
        for k in range(count):
            refs[2 * count + n][k] = refs[n * count + k][...]


def stack_lines(first, second):
    shape = (len(first), *first[0].shape)
    return pl.pallas_call(
        stack_kernel,
        out_shape=(jax.ShapeDtypeStruct(shape, first[0].dtype),) * 2,
        in_specs=[VMEM] * (2 * len(first)),
        out_specs=(VMEM,) * 2,
        compiler_params=pltpu.CompilerParams(vmem_limit_bytes=VMEM_LIMIT),
        cost_estimate=cost(0, 8 * math.prod(shape)),
        name="stack_lines",
    )(*first, *second)


def unpack_weight_kernel(chips, place_ref, own_ref, other_ref, out_ref):
    for ref, core in ((own_ref, place_ref[2]), (other_ref, 1 - place_ref[2])):
        for i, column in enumerate(core_columns(core, chips)):
            out_ref[:, pl.ds(column, TILE)] = ref[:, pl.ds(i * TILE, TILE)].astype(F32)


def unpack_weight(place, own, other, chips):
    rows, columns = own.shape
    return pl.pallas_call(
        functools.partial(unpack_weight_kernel, chips),
        out_shape=jax.ShapeDtypeStruct((rows, 2 * columns), F32),
        in_specs=[SMEM, VMEM, VMEM],
        out_specs=VMEM,
        compiler_params=pltpu.CompilerParams(vmem_limit_bytes=VMEM_LIMIT),
        cost_estimate=cost(0, 12 * rows * columns),
        name="unpack_weight",
    )(place, own, other)


def slot_plan(place_ref, tiles_ref, counts_ref, unit, slot, units, width):
    first_head = place_ref[0]
    split = counts_ref[first_head * units + unit]
    in_first = slot < split
    head = jnp.where(in_first, first_head, first_head + place_ref[1])
    entry = jnp.minimum(jnp.where(in_first, slot, width - slot), width - 1)
    tile = tiles_ref[(head * units + unit) * width + entry]
    return in_first, jnp.where(in_first, 0, 1), tile


def rows_of(ref, half, tile):
    per_block = ref.shape[2] // TILE
    start = pl.multiple_of(lax.rem(tile, per_block) * TILE, TILE)
    return ref.at[lax.div(tile, per_block), half, pl.ds(start, TILE), :]


def forward_kernel(multi, slots, units, width, scale, place_ref, tiles_ref, counts_ref, qkv_ref, a_ref, lse_ref, *refs):
    block_refs, (vt_ref, s_ref, p_ref) = refs[:-3], refs[-3:]
    scale2 = scale * math.log2(math.e)
    q_ref, k_ref, v_ref = (qkv_ref.at[:, n] for n in range(3))

    @pl.loop(0, units, unroll=2)
    def _(t):
        for half in range(2):
            vt_ref[half * units + t] = rows_of(v_ref, half, t)[...].T

    @pl.loop(0, units // multi)
    def _(step):
        plans = [[slot_plan(place_ref, tiles_ref, counts_ref, step * multi + u, j, units, width) for j in range(slots)] for u in range(multi)]
        all_tops = []
        for u in range(multi):
            tops = []
            for j, (in_first, half, tile) in enumerate(plans[u]):
                s = mm(rows_of(k_ref, half, tile)[...], rows_of(q_ref, half, step * multi + u)[...], NT)
                s_ref[u * slots + j] = s
                tops.append(jnp.max(s.reshape(TILE // 8, 8, TILE), axis=0))
            all_tops.append(tops)
        low = jnp.full((8, TILE), -jnp.inf, F32)
        zero = jnp.zeros((TILE, TILE), BF16)
        stats = []
        for u in range(multi):
            top = []
            for half in range(2):
                m = low
                for (in_first, _, _), t8 in zip(plans[u], all_tops[u]):
                    use = in_first if half == 0 else jnp.logical_not(in_first)
                    m = jnp.maximum(m, jnp.where(use, t8, low))
                top.append(jnp.max(m, axis=0, keepdims=True) * scale2)
            totals = [jnp.zeros((8, TILE), F32)] * 2
            for j, (in_first, half, tile) in enumerate(plans[u]):
                p = jnp.exp2(s_ref[u * slots + j] * scale2 - jnp.where(in_first, top[0], top[1]))
                l8 = jnp.sum(p.reshape(TILE // 8, 8, TILE), axis=0)
                totals[0] = totals[0] + jnp.where(in_first, l8, 0.0)
                totals[1] = totals[1] + jnp.where(in_first, 0.0, l8)
                pb = p.astype(BF16)
                p_ref[u, pl.ds(j * TILE, TILE), 0:TILE] = jnp.where(in_first, pb, zero)
                p_ref[u, pl.ds(j * TILE, TILE), TILE : 2 * TILE] = jnp.where(in_first, zero, pb)
            stats.append((top, totals))
        for u in range(multi):
            unit = step * multi + u
            top, totals = stats[u]
            vt = jnp.concatenate([vt_ref[half * units + tile] for _, half, tile in plans[u]], axis=1)
            mixed = mm(vt, p_ref[u])
            for half in range(2):
                total = jnp.sum(totals[half], axis=0, keepdims=True)
                a_t = mixed[:, half * TILE : (half + 1) * TILE] / total
                rows_of(a_ref, half, unit)[...] = a_t.T.astype(BF16)
                lse_ref[half * units + unit] = jnp.broadcast_to(top[half] + jnp.log2(total), (8, TILE))

    chips = len(block_refs)
    for k, ref in enumerate(block_refs):
        ref[...] = a_ref[lax.rem(place_ref[5] + k, chips)]


def attention_forward(place, tiles, counts, qkv, chips, width):
    seq, _, halves, tokens, head_dim = qkv.shape
    units = seq * tokens // TILE
    slots = width + 1
    rows = seq * tokens // chips
    return pl.pallas_call(
        functools.partial(forward_kernel, UNITS_AT_ONCE, slots, units, width, 1.0 / math.sqrt(head_dim)),
        out_shape=(
            jax.ShapeDtypeStruct((chips, halves, rows, head_dim), BF16),
            jax.ShapeDtypeStruct((halves * units, 8, TILE), F32),
        )
        + (jax.ShapeDtypeStruct((halves, rows, head_dim), BF16),) * chips,
        in_specs=[SMEM] * 3 + [VMEM],
        out_specs=(VMEM,) * (2 + chips),
        scratch_shapes=[
            pltpu.VMEM((halves * units, head_dim, TILE), BF16),
            pltpu.VMEM((UNITS_AT_ONCE * slots, TILE, TILE), F32),
            pltpu.VMEM((UNITS_AT_ONCE, slots * TILE, 2 * TILE), BF16),
        ],
        compiler_params=pltpu.CompilerParams(vmem_limit_bytes=20 * MIB),
        cost_estimate=cost(3*10**11, MIB),
        name="attention_forward",
    )(place, tiles, counts, qkv)


def backward_kernel(multi, slots, units, width, scale, place_ref, tiles_ref, counts_ref, qkv_ref, g_ref, a_ref, lse_ref, *refs):
    out_ref, kt_ref, dk_acc, dv_acc, s_ref, dp_ref, p_ref, d_ref = refs[-12:-4]
    loads = [pltpu.make_async_copy(ref, refs[n - 4], refs[-1].at[n]) for n, ref in enumerate((g_ref, a_ref, lse_ref))]
    for load in loads:
        load.start()
    g_ref, a_ref, lse_ref = refs[-4:-1]
    scale2 = scale * math.log2(math.e)
    q_ref, k_ref, v_ref = (qkv_ref.at[:, n] for n in range(3))
    dq_ref, dk_ref, dv_ref = (out_ref.at[:, n] for n in range(3))

    @pl.loop(0, units, unroll=2)
    def _(t):
        for half in range(2):
            kt_ref[half * units + t] = rows_of(k_ref, half, t)[...].T
            dk_acc[half * units + t] = jnp.zeros((TILE, TILE), F32)
            dv_acc[half * units + t] = jnp.zeros((TILE, TILE), F32)

    for load in loads:
        load.wait()

    @pl.loop(0, units // multi)
    def _(step):
        plans = [[slot_plan(place_ref, tiles_ref, counts_ref, step * multi + u, j, units, width) for j in range(slots)] for u in range(multi)]
        zero = jnp.zeros((TILE, TILE), BF16)
        deltas, lses = [], []
        for u in range(multi):
            unit = step * multi + u
            delta, lse = [], []
            for half in range(2):
                prod = rows_of(g_ref, half, unit)[...].astype(F32) * rows_of(a_ref, half, unit)[...].astype(F32)
                delta.append(jnp.sum(prod.T, axis=0, keepdims=True))
                lse.append(lse_ref[half * units + unit][0:1])
            deltas.append(delta)
            lses.append(lse)
            for j, (in_first, half, tile) in enumerate(plans[u]):
                s_ref[u * slots + j] = mm(rows_of(k_ref, half, tile)[...], rows_of(q_ref, half, unit)[...], NT)
                dp_ref[u * slots + j] = mm(rows_of(v_ref, half, tile)[...], rows_of(g_ref, half, unit)[...], NT)
        for u in range(multi):
            for j, (in_first, half, tile) in enumerate(plans[u]):
                p = jnp.exp2(s_ref[u * slots + j] * scale2 - jnp.where(in_first, lses[u][0], lses[u][1]))
                ds = (p * (dp_ref[u * slots + j] - jnp.where(in_first, deltas[u][0], deltas[u][1]))).astype(BF16)
                p_ref[u * slots + j] = p.astype(BF16)
                d_ref[u, pl.ds(j * TILE, TILE), 0:TILE] = jnp.where(in_first, ds, zero)
                d_ref[u, pl.ds(j * TILE, TILE), TILE : 2 * TILE] = jnp.where(in_first, zero, ds)
        for u in range(multi):
            unit = step * multi + u
            for j, (in_first, half, tile) in enumerate(plans[u]):
                ds = d_ref[u, pl.ds(j * TILE, TILE), pl.ds(pl.multiple_of(half * TILE, TILE), TILE)]
                dv_acc[half * units + tile] += mm(p_ref[u * slots + j], rows_of(g_ref, half, unit)[...])
                dk_acc[half * units + tile] += mm(ds, rows_of(q_ref, half, unit)[...])
            kt = jnp.concatenate([kt_ref[half * units + tile] for _, half, tile in plans[u]], axis=1)
            dq_t = mm(kt, d_ref[u]) * scale
            for half in range(2):
                rows_of(dq_ref, half, unit)[...] = dq_t[:, half * TILE : (half + 1) * TILE].T.astype(BF16)

    @pl.loop(0, units, unroll=2)
    def _(t):
        for half in range(2):
            rows_of(dk_ref, half, t)[...] = (dk_acc[half * units + t] * scale).astype(BF16)
            rows_of(dv_ref, half, t)[...] = dv_acc[half * units + t].astype(BF16)


def attention_backward(place, tiles, counts, qkv, g, a, lse, after, width):
    seq, _, halves, tokens, head_dim = qkv.shape
    units = seq * tokens // TILE
    slots = width + 1
    return pl.pallas_call(
        functools.partial(backward_kernel, UNITS_AT_ONCE, slots, units, width, 1.0 / math.sqrt(head_dim)),
        out_shape=jax.ShapeDtypeStruct(qkv.shape, BF16),
        in_specs=[SMEM] * 3 + [VMEM] + [HBM] * (3 + len(after)),
        out_specs=VMEM,
        scratch_shapes=[
            pltpu.VMEM((halves * units, head_dim, TILE), BF16),
            pltpu.VMEM((halves * units, TILE, head_dim), F32),
            pltpu.VMEM((halves * units, TILE, head_dim), F32),
            pltpu.VMEM((UNITS_AT_ONCE * slots, TILE, TILE), F32),
            pltpu.VMEM((UNITS_AT_ONCE * slots, TILE, TILE), F32),
            pltpu.VMEM((UNITS_AT_ONCE * slots, TILE, TILE), BF16),
            pltpu.VMEM((UNITS_AT_ONCE, slots * TILE, 2 * TILE), BF16),
            pltpu.VMEM(g.shape, g.dtype),
            pltpu.VMEM(a.shape, a.dtype),
            pltpu.VMEM(lse.shape, lse.dtype),
            pltpu.SemaphoreType.DMA((3,)),
        ],
        compiler_params=pltpu.CompilerParams(vmem_limit_bytes=VMEM_LIMIT),
        cost_estimate=cost(3*10**11, MIB),
        name="attention_backward",
    )(place, tiles, counts, qkv, g, a, lse, *after)


def block_row(place_ref, side, ky, kz):
    y = lax.rem(place_ref[3] + side - ky, side)
    z = lax.rem(place_ref[4] + side - kz, side)
    return pl.multiple_of((y * side + z) * TILE, TILE)


def grad_attn_kernel(side, chips, place_ref, own_ref, other_ref, *refs):
    w_refs, g_ref = refs[: 2 * side], refs[-1]
    tokens = own_ref.shape[0]
    core = place_ref[2]
    for part in range(2):
        total = None
        for i in range(side):
            starts = [block_row(place_ref, side, *((i, j) if part == 0 else (j, i))) for j in range(side)]
            rows = [jnp.concatenate([ref[:, pl.ds(start, TILE)] for start in starts], axis=1) for ref in (own_ref, other_ref)]
            w = w_refs[part * side + i][...]
            step = mm(jnp.concatenate(rows, axis=0), w.reshape(side * TILE, w.shape[2]))
            total = step if total is None else total + step
        g = total.astype(BF16)
        for n in range(chips):
            x, half = divmod(part * chips + n, 2)
            for slot, first in ((core, 0), (1 - core, tokens)):
                target = pl.ds(pl.multiple_of(slot * tokens, tokens), tokens)
                g_ref[x, half, target, :] = g[first : first + tokens, n * TILE : (n + 1) * TILE]


def grad_attn(place, own, other, weights, after, side, chips):
    tokens, depth = own.shape
    columns = 2 * weights[0].shape[2]
    return pl.pallas_call(
        functools.partial(grad_attn_kernel, side, chips),
        out_shape=jax.ShapeDtypeStruct((chips, 2, 2 * tokens, TILE), BF16),
        in_specs=[SMEM] + [VMEM] * (2 + len(weights)) + [HBM],
        out_specs=VMEM,
        compiler_params=pltpu.CompilerParams(vmem_limit_bytes=VMEM_LIMIT),
        cost_estimate=cost(4 * tokens * depth * columns, 7 * MIB),
        name="grad_attn",
    )(place, own, other, *weights, after)


def row_copies(place_ref, block_refs, rows_ref, sems):
    chips = len(block_refs)
    halves, rows, width = block_refs[0].shape
    tokens = rows // 2
    core = place_ref[2]
    copies = []
    for k, ref in enumerate(block_refs):
        chip = lax.rem(place_ref[5] + chips - k, chips)
        for half in range(halves):
            target = pl.ds(pl.multiple_of((chip * halves + half) * width, width), width)
            for slot, first in ((core, 0), (1 - core, tokens)):
                source = ref.at[half, pl.ds(pl.multiple_of(slot * tokens, tokens), tokens), :]
                copies.append(pltpu.make_async_copy(source, rows_ref.at[pl.ds(first, tokens), target], sems.at[len(copies)]))
    return copies


def project_kernel(side, place_ref, *refs):
    block_refs, w_refs, (own_ref, other_ref, rows_ref, sems) = refs[: -5 - 2 * side], refs[-5 - 2 * side : -5], refs[-4:]
    copies = row_copies(place_ref, block_refs, rows_ref, sems)
    for copy in copies:
        copy.start()
    for copy in copies:
        copy.wait()
    tokens = own_ref.shape[0]
    for ky in range(side):
        for kz in range(0, side, 2):
            first = w_refs[ky][kz : kz + 2]
            second = jnp.concatenate([w_refs[side + kz][ky], w_refs[side + kz + 1][ky]], axis=0)
            w = jnp.concatenate([first.reshape(second.shape), second], axis=1)
            out = mm(rows_ref[...], w, NT)
            for n in range(2):
                target = pl.ds(block_row(place_ref, side, ky, kz + n), TILE)
                block = out[:, n * TILE : (n + 1) * TILE]
                own_ref[:, target] = block[:tokens]
                other_ref[:, target] = block[tokens:].astype(BF16)


def project(place, blocks, weights, after, side):
    features = side * side * weights[0].shape[1]
    columns = 2 * weights[0].shape[2]
    tokens = blocks[0].shape[1] // 2
    return pl.pallas_call(
        functools.partial(project_kernel, side),
        out_shape=(jax.ShapeDtypeStruct((tokens, features), F32), jax.ShapeDtypeStruct((tokens, features), BF16)),
        in_specs=[SMEM] + [HBM] * len(blocks) + [VMEM] * len(weights) + [HBM],
        out_specs=(VMEM, VMEM),
        scratch_shapes=[pltpu.VMEM((2 * tokens, columns), BF16), pltpu.SemaphoreType.DMA((4 * len(blocks),))],
        compiler_params=pltpu.CompilerParams(vmem_limit_bytes=VMEM_LIMIT),
        cost_estimate=cost(4 * tokens * features * columns, 8 * MIB),
        name="project",
    )(place, *blocks, *weights, after)


def grad_weight_kernel(side, chips, place_ref, own_ref, other_ref, *refs):
    block_refs, out_refs, (rows_ref, grad_ref, part_ref, sems, load_sems) = refs[:chips], refs[chips:-5], refs[-5:]
    tokens = own_ref.shape[0]
    loads = row_copies(place_ref, block_refs, rows_ref, load_sems)
    for n, ref in enumerate((own_ref, other_ref)):
        target = grad_ref.at[pl.ds(n * tokens, tokens), :]
        loads.append(pltpu.make_async_copy(ref, target, load_sems.at[len(loads)]))
    for load in loads:
        load.start()
    for load in loads:
        load.wait()
    rows = part_ref.shape[2]
    half = part_ref.shape[3]
    copies = [pltpu.make_async_copy(part_ref.at[n], out_refs[n], sems.at[n]) for n in range(2 * side)]
    for ky in range(side):
        for kz in range(side):
            row = lax.rem(place_ref[3] + ky, side) * side + lax.rem(place_ref[4] + kz, side)
            columns = pl.ds(pl.multiple_of(row * rows, rows), rows)
            part = mm(grad_ref[:, columns], rows_ref[...], TN)
            part_ref[kz, ky] = part[:, :half].astype(BF16)
            part_ref[side + ky, kz] = part[:, half:].astype(BF16)
            if ky == side - 1:
                copies[kz].start()
        copies[side + ky].start()
    for copy in copies:
        copy.wait()


def grad_weight_parts(place, own, other, blocks, side):
    tokens, features = own.shape
    chips = len(blocks)
    columns = chips * blocks[0].shape[0] * blocks[0].shape[2]
    rows = features // side**2
    return pl.pallas_call(
        functools.partial(grad_weight_kernel, side, chips),
        out_shape=(jax.ShapeDtypeStruct((side, rows, columns // 2), BF16),) * (2 * side),
        in_specs=[SMEM] + [HBM] * (2 + chips),
        out_specs=(HBM,) * (2 * side),
        scratch_shapes=[
            pltpu.VMEM((2 * tokens, columns), BF16),
            pltpu.VMEM((2 * tokens, features), BF16),
            pltpu.VMEM((2 * side, side, rows, columns // 2), BF16),
            pltpu.SemaphoreType.DMA((2 * side,)),
            pltpu.SemaphoreType.DMA((4 * chips + 2,)),
        ],
        compiler_params=pltpu.CompilerParams(vmem_limit_bytes=VMEM_LIMIT),
        cost_estimate=cost(4 * tokens * features * columns, 7 * MIB),
        name="grad_weight_parts",
    )(place, own, other, *blocks)


def gate_kernel(*refs):
    del refs


def gate(values, *after):
    return pl.pallas_call(
        gate_kernel,
        out_shape=jax.ShapeDtypeStruct(values.shape, values.dtype),
        in_specs=[HBM] * (1 + len(after)),
        out_specs=HBM,
        input_output_aliases={0: 0},
        compiler_params=pltpu.CompilerParams(vmem_limit_bytes=VMEM_LIMIT),
        name="gate",
    )(values, *after)


def sum_kernel(*refs):
    side = len(refs) // 4
    for n in range(2):
        in_refs = refs[n * side : (n + 1) * side]
        for k in range(side):
            total = in_refs[0][k].astype(F32)
            for ref in in_refs[1:]:
                total = total + ref[k].astype(F32)
            refs[2 * side + n * side + k][...] = total.astype(BF16)


def summed(first, second):
    side, rows, width = first[0].shape
    sums = pl.pallas_call(
        sum_kernel,
        out_shape=(jax.ShapeDtypeStruct((rows, width), BF16),) * (2 * side),
        in_specs=[VMEM] * (2 * side),
        out_specs=(VMEM,) * (2 * side),
        compiler_params=pltpu.CompilerParams(vmem_limit_bytes=VMEM_LIMIT),
        cost_estimate=cost(10**12, MIB),
        name="summed",
    )(*first, *second)
    return sums[:side], sums[side:]


def sum_pair_kernel(*refs):
    out_ref = refs[-1]
    count = len(refs) // 2
    width = refs[0].shape[1]
    for side in range(2):
        total = refs[side * count][...].astype(F32)
        for ref in refs[side * count + 1 : (side + 1) * count]:
            total = total + ref[...].astype(F32)
        out_ref[:, side * width : (side + 1) * width] = total.astype(BF16)


def summed_side_by_side(first, second):
    rows, width = first[0].shape
    return pl.pallas_call(
        sum_pair_kernel,
        out_shape=jax.ShapeDtypeStruct((rows, 2 * width), BF16),
        in_specs=[VMEM] * (2 * len(first)),
        out_specs=VMEM,
        compiler_params=pltpu.CompilerParams(vmem_limit_bytes=VMEM_LIMIT),
        cost_estimate=cost(0, 4 * (len(first) + 1) * rows * width),
        name="summed_side_by_side",
    )(*first, *second)


def sum_chips_kernel(a_ref, b_ref, c_ref, d_ref, *refs):
    first = a_ref[...].astype(F32) + b_ref[...].astype(F32)
    second = c_ref[...].astype(F32) + d_ref[...].astype(F32)
    refs[-1][...] = (first + second).astype(BF16)


def summed_over_chips(parts, after):
    return pl.pallas_call(
        sum_chips_kernel,
        out_shape=jax.ShapeDtypeStruct(parts[0].shape, BF16),
        in_specs=[VMEM] * len(parts) + [HBM] * len(after),
        out_specs=VMEM,
        compiler_params=pltpu.CompilerParams(vmem_limit_bytes=VMEM_LIMIT),
        cost_estimate=cost(0, 10 * math.prod(parts[0].shape)),
        name="summed_over_chips",
    )(*parts, *after)


def per_device(queries, key_states, value_states, grad_output, out_weight, key_tiles, tile_count):
    seq = lax.axis_size("seq")
    ranks = lax.axis_size("dp")
    side = math.isqrt(ranks)
    chips = seq // 2
    s_index = lax.axis_index("seq")
    d_index = lax.axis_index("dp")
    core = lax.rem(s_index, 2)
    tokens, columns = queries.shape[1:]
    heads, units, width = key_tiles.shape[1:]
    head_dim = columns // heads
    rows = out_weight.shape[0]
    place = jnp.stack([s_index, jnp.int32(seq), core, lax.div(d_index, side), lax.rem(d_index, side), lax.div(s_index, 2)]).astype(jnp.int32)
    lists = key_tiles.reshape(-1)
    counts = tile_count.reshape(-1)
    same_core = [list(range(c, seq, 2)) for c in range(2)]
    across = [(i, i ^ 1) for i in range(seq)]

    def y_shift(k):
        return [(i, (i // side + k) % side * side + i % side) for i in range(ranks)]

    def z_shift(k):
        return [(i, i // side * side + (i % side + k) % side) for i in range(ranks)]

    def x_shift(k):
        return [(i, (i + 2 * k) % seq) for i in range(seq)]

    def x_swap(k):
        return [(i, i ^ (2 * k)) for i in range(seq)]

    def over_chips(values):
        return lax.all_to_all(values, "seq", split_axis=0, concat_axis=0, tiled=True, axis_index_groups=same_core)

    shard_z, shard_y = pack_weight(place, out_weight, chips)
    lines_z, lines_y = stack_lines(
        [shard_z] + [lax.ppermute(shard_z, "dp", z_shift(k)) for k in range(1, side)],
        [shard_y] + [lax.ppermute(shard_y, "dp", y_shift(k)) for k in range(1, side)],
    )
    weights = [lines_z] + [lax.ppermute(lines_z, "dp", y_shift(k)) for k in range(1, side)]
    weights += [lines_y] + [lax.ppermute(lines_y, "dp", z_shift(k)) for k in range(1, side)]
    packed = pack(queries, key_states, value_states, seq, head_dim)
    qkv = lax.all_to_all(packed, "seq", split_axis=0, concat_axis=0, tiled=True)
    own_rows = grad_output[0]
    other_rows = lax.ppermute(own_rows, "seq", across)
    a, lse, *a_blocks = attention_forward(place, lists, counts, qkv, chips, width)
    a_home = [a_blocks[0]] + [lax.ppermute(a_blocks[k], "seq", x_shift(k)) for k in range(1, chips)]
    g = over_chips(gate(grad_attn(place, own_rows, other_rows, weights, lse, side, chips), *a_home))
    parts = grad_weight_parts(place, own_rows, other_rows, a_home, side)
    z_first = [parts[0]] + [lax.ppermute(parts[k], "dp", z_shift(k)) for k in range(1, side)]
    y_first = [parts[side]] + [lax.ppermute(parts[side + k], "dp", y_shift(k)) for k in (1, side - 1)]
    grads = attention_backward(place, lists, counts, qkv, g, a, lse, (parts[0],), width)
    grads_home = lax.all_to_all(grads, "seq", split_axis=0, concat_axis=0, tiled=True)
    y_first += [lax.ppermute(gate(parts[side + k], grads), "dp", y_shift(k)) for k in range(2, side - 1)]

    z_sum, y_sum = summed(z_first, y_first)
    out_own, out_other = project(place, a_home, weights, grads, side)
    output = (out_own + lax.ppermute(out_other, "seq", across).astype(F32)).astype(BF16)
    chip_share = summed_side_by_side(
        [z_sum[0]] + [lax.ppermute(z_sum[k], "dp", y_shift(k)) for k in range(1, side)],
        [y_sum[0]] + [lax.ppermute(y_sum[k], "dp", z_shift(k)) for k in range(1, side)],
    )
    grad_query, grad_key, grad_value = unpack(grads_home)
    by_chip = [chip_share] + [lax.ppermute(chip_share, "seq", x_swap(k)) for k in range(1, chips)]
    own_half = summed_over_chips(by_chip, (grad_query, output))
    grad_weight = unpack_weight(place, own_half, lax.ppermute(own_half, "seq", across), chips)
    return output[None], grad_query, grad_key, grad_value, grad_weight


def solution(mesh):
    in_specs = (
        P("dp", "seq", None),
        P("dp", "seq", None),
        P("dp", "seq", None),
        P("dp", "seq", None),
        P("dp", None),
        P("dp", None, None, None),
        P("dp", None, None),
    )
    out_specs = (
        P("dp", "seq", None),
        P("dp", "seq", None),
        P("dp", "seq", None),
        P("dp", "seq", None),
        P("dp", None),
    )
    return jax.shard_map(per_device, mesh=mesh, in_specs=in_specs, out_specs=out_specs, check_vma=False)
```

```python
import functools
import math

import jax
import jax.numpy as jnp
from jax import lax
from jax.experimental import pallas as pl
from jax.experimental.pallas import tpu as pltpu
from jax.sharding import PartitionSpec as P

NN = (((1,), (0,)), ((), ()))
NT = (((1,), (1,)), ((), ()))
TN = (((0,), (0,)), ((), ()))
F32 = jnp.float32
BF16 = jnp.bfloat16
MIB = 2**20
SMEM = pl.BlockSpec(memory_space=pltpu.SMEM)
VMEM = pl.BlockSpec(memory_space=pltpu.VMEM)
ANY = pl.BlockSpec(memory_space=pl.ANY)
HBM = pl.BlockSpec(memory_space=pltpu.HBM)
TILE = 128
UNITS_AT_ONCE = 8
VMEM_LIMIT = 60 * MIB


def mm(a, b, dims=NN):
    return lax.dot_general(a, b, dims, preferred_element_type=F32)


def cost(flops, moved, exps=0):
    return pl.CostEstimate(flops=flops, bytes_accessed=moved, transcendentals=exps)


def pack_kernel(q_ref, k_ref, v_ref, out_ref, rows_ref, in_sems, out_sems):
    seq, _, halves, _, width = out_ref.shape
    loads = [pltpu.make_async_copy(ref.at[0], rows_ref.at[n], in_sems.at[n]) for n, ref in enumerate((q_ref, k_ref, v_ref))]
    for load in loads:
        load.start()
    stores = []
    for n, load in enumerate(loads):
        load.wait()
        for s in range(seq):
            for half in range(halves):
                source = rows_ref.at[n, :, pl.ds((s + seq * half) * width, width)]
                stores.append(pltpu.make_async_copy(source, out_ref.at[s, n, half], out_sems.at[len(stores)]))
                stores[-1].start()
    for store in stores:
        store.wait()


def pack(q, k, v, seq, head_dim):
    _, tokens, columns = q.shape
    halves = columns // (seq * head_dim)
    return pl.pallas_call(
        pack_kernel,
        out_shape=jax.ShapeDtypeStruct((seq, 3, halves, tokens, head_dim), q.dtype),
        in_specs=[HBM] * 3,
        out_specs=HBM,
        scratch_shapes=[
            pltpu.VMEM((3, tokens, columns), q.dtype),
            pltpu.SemaphoreType.DMA((3,)),
            pltpu.SemaphoreType.DMA((3 * seq * halves,)),
        ],
        compiler_params=pltpu.CompilerParams(vmem_limit_bytes=VMEM_LIMIT),
        cost_estimate=cost(0, 12 * tokens * columns),
        name="pack_heads",
    )(q, k, v)


def unpack_kernel(in_ref, q_ref, k_ref, v_ref):
    seq, _, halves, _, width = in_ref.shape
    for n, ref in enumerate((q_ref, k_ref, v_ref)):
        for s in range(seq):
            for half in range(halves):
                column = (s + seq * half) * width
                ref[0, :, column : column + width] = in_ref[s, n, half]


def unpack(blocks):
    seq, _, halves, tokens, head_dim = blocks.shape
    columns = seq * halves * head_dim
    rows = tokens // 4
    return pl.pallas_call(
        unpack_kernel,
        grid=(tokens // rows,),
        out_shape=(jax.ShapeDtypeStruct((1, tokens, columns), blocks.dtype),) * 3,
        in_specs=[pl.BlockSpec((seq, 3, halves, rows, head_dim), lambda i: (0, 0, 0, i, 0))],
        out_specs=(pl.BlockSpec((1, rows, columns), lambda i: (0, i, 0)),) * 3,
        compiler_params=pltpu.CompilerParams(vmem_limit_bytes=VMEM_LIMIT),
        cost_estimate=cost(0, 12 * tokens * columns),
        name="unpack_heads",
    )(blocks)


def core_columns(core, chips):
    return [pl.multiple_of((2 * x + core + 2 * chips * half) * TILE, TILE) for x in range(chips) for half in range(2)]


def pack_weight_kernel(chips, place_ref, in_ref, *out_refs):
    for i, column in enumerate(core_columns(place_ref[2], chips)):
        out_refs[i // chips][:, pl.ds(i % chips * TILE, TILE)] = in_ref[:, pl.ds(column, TILE)]


def pack_weight(place, shard, chips):
    rows, columns = shard.shape
    return pl.pallas_call(
        functools.partial(pack_weight_kernel, chips),
        out_shape=(jax.ShapeDtypeStruct((rows, columns // 4), shard.dtype),) * 2,
        in_specs=[SMEM, VMEM],
        out_specs=(VMEM,) * 2,
        compiler_params=pltpu.CompilerParams(vmem_limit_bytes=VMEM_LIMIT),
        cost_estimate=cost(0, 3 * rows * columns),
        name="pack_weight",
    )(place, shard)


def stack_kernel(*refs):
    count = len(refs) // 2 - 1
    for n in range(2):
        for k in range(count):
            refs[2 * count + n][k] = refs[n * count + k][...]


def stack_lines(first, second):
    shape = (len(first), *first[0].shape)
    return pl.pallas_call(
        stack_kernel,
        out_shape=(jax.ShapeDtypeStruct(shape, first[0].dtype),) * 2,
        in_specs=[VMEM] * (2 * len(first)),
        out_specs=(VMEM,) * 2,
        compiler_params=pltpu.CompilerParams(vmem_limit_bytes=VMEM_LIMIT),
        cost_estimate=cost(0, 8 * math.prod(shape)),
        name="stack_lines",
    )(*first, *second)


def unpack_weight_kernel(chips, place_ref, own_ref, other_ref, out_ref):
    for ref, core in ((own_ref, place_ref[2]), (other_ref, 1 - place_ref[2])):
        for i, column in enumerate(core_columns(core, chips)):
            out_ref[:, pl.ds(column, TILE)] = ref[:, pl.ds(i * TILE, TILE)].astype(F32)


def unpack_weight(place, own, other, chips):
    rows, columns = own.shape
    return pl.pallas_call(
        functools.partial(unpack_weight_kernel, chips),
        out_shape=jax.ShapeDtypeStruct((rows, 2 * columns), F32),
        in_specs=[SMEM, VMEM, VMEM],
        out_specs=VMEM,
        compiler_params=pltpu.CompilerParams(vmem_limit_bytes=VMEM_LIMIT),
        cost_estimate=cost(0, 12 * rows * columns),
        name="unpack_weight",
    )(place, own, other)


def slot_plan(place_ref, tiles_ref, counts_ref, unit, slot, units, width):
    first_head = place_ref[0]
    split = counts_ref[first_head * units + unit]
    in_first = slot < split
    head = jnp.where(in_first, first_head, first_head + place_ref[1])
    entry = jnp.minimum(jnp.where(in_first, slot, width - slot), width - 1)
    tile = tiles_ref[(head * units + unit) * width + entry]
    return in_first, jnp.where(in_first, 0, 1), tile


def rows_of(ref, half, tile):
    per_block = ref.shape[2] // TILE
    start = pl.multiple_of(lax.rem(tile, per_block) * TILE, TILE)
    return ref.at[lax.div(tile, per_block), half, pl.ds(start, TILE), :]


def forward_kernel(multi, slots, units, width, scale, place_ref, tiles_ref, counts_ref, qkv_ref, a_ref, lse_ref, *refs):
    block_refs, (vt_ref, s_ref, p_ref) = refs[:-3], refs[-3:]
    scale2 = scale * math.log2(math.e)
    q_ref, k_ref, v_ref = (qkv_ref.at[:, n] for n in range(3))

    @pl.loop(0, units, unroll=2)
    def _(t):
        for half in range(2):
            vt_ref[half * units + t] = rows_of(v_ref, half, t)[...].T

    @pl.loop(0, units // multi)
    def _(step):
        plans = [[slot_plan(place_ref, tiles_ref, counts_ref, step * multi + u, j, units, width) for j in range(slots)] for u in range(multi)]
        all_tops = []
        for u in range(multi):
            tops = []
            for j, (in_first, half, tile) in enumerate(plans[u]):
                s = mm(rows_of(k_ref, half, tile)[...], rows_of(q_ref, half, step * multi + u)[...], NT)
                s_ref[u * slots + j] = s
                tops.append(jnp.max(s.reshape(TILE // 8, 8, TILE), axis=0))
            all_tops.append(tops)
        low = jnp.full((8, TILE), -jnp.inf, F32)
        zero = jnp.zeros((TILE, TILE), BF16)
        stats = []
        for u in range(multi):
            top = []
            for half in range(2):
                m = low
                for (in_first, _, _), t8 in zip(plans[u], all_tops[u]):
                    use = in_first if half == 0 else jnp.logical_not(in_first)
                    m = jnp.maximum(m, jnp.where(use, t8, low))
                top.append(jnp.max(m, axis=0, keepdims=True) * scale2)
            totals = [jnp.zeros((8, TILE), F32)] * 2
            for j, (in_first, half, tile) in enumerate(plans[u]):
                p = jnp.exp2(s_ref[u * slots + j] * scale2 - jnp.where(in_first, top[0], top[1]))
                l8 = jnp.sum(p.reshape(TILE // 8, 8, TILE), axis=0)
                totals[0] = totals[0] + jnp.where(in_first, l8, 0.0)
                totals[1] = totals[1] + jnp.where(in_first, 0.0, l8)
                pb = p.astype(BF16)
                p_ref[u, pl.ds(j * TILE, TILE), 0:TILE] = jnp.where(in_first, pb, zero)
                p_ref[u, pl.ds(j * TILE, TILE), TILE : 2 * TILE] = jnp.where(in_first, zero, pb)
            stats.append((top, totals))
        for u in range(multi):
            unit = step * multi + u
            top, totals = stats[u]
            vt = jnp.concatenate([vt_ref[half * units + tile] for _, half, tile in plans[u]], axis=1)
            mixed = mm(vt, p_ref[u])
            for half in range(2):
                total = jnp.sum(totals[half], axis=0, keepdims=True)
                a_t = mixed[:, half * TILE : (half + 1) * TILE] / total
                rows_of(a_ref, half, unit)[...] = a_t.T.astype(BF16)
                lse_ref[half * units + unit] = jnp.broadcast_to(top[half] + jnp.log2(total), (8, TILE))

    chips = len(block_refs) + 1
    for k, ref in enumerate(block_refs, 1):
        ref[...] = a_ref[lax.rem(place_ref[5] + k, chips)]


def attention_forward(place, tiles, counts, qkv, chips, width):
    seq, _, halves, tokens, head_dim = qkv.shape
    units = seq * tokens // TILE
    slots = width + 1
    rows = seq * tokens // chips
    return pl.pallas_call(
        functools.partial(forward_kernel, UNITS_AT_ONCE, slots, units, width, 1.0 / math.sqrt(head_dim)),
        out_shape=(
            jax.ShapeDtypeStruct((chips, halves, rows, head_dim), BF16),
            jax.ShapeDtypeStruct((halves * units, 8, TILE), F32),
        )
        + (jax.ShapeDtypeStruct((halves, rows, head_dim), BF16),) * (chips - 1),
        in_specs=[SMEM] * 3 + [VMEM],
        out_specs=(VMEM,) * (1 + chips),
        scratch_shapes=[
            pltpu.VMEM((halves * units, head_dim, TILE), BF16),
            pltpu.VMEM((UNITS_AT_ONCE * slots, TILE, TILE), F32),
            pltpu.VMEM((UNITS_AT_ONCE, slots * TILE, 2 * TILE), BF16),
        ],
        compiler_params=pltpu.CompilerParams(vmem_limit_bytes=28 * MIB),
        cost_estimate=cost(3*10**11, MIB),
        name="attention_forward",
    )(place, tiles, counts, qkv)


def backward_kernel(multi, slots, units, width, scale, place_ref, tiles_ref, counts_ref, qkv_ref, g_ref, a_ref, lse_ref, *refs):
    out_ref, kt_ref, dk_acc, dv_acc, s_ref, dp_ref, p_ref, d_ref = refs[-12:-4]
    loads = [pltpu.make_async_copy(ref, refs[n - 4], refs[-1].at[n]) for n, ref in enumerate((g_ref, a_ref, lse_ref))]
    for load in loads:
        load.start()
    g_ref, a_ref, lse_ref = refs[-4:-1]
    scale2 = scale * math.log2(math.e)
    q_ref, k_ref, v_ref = (qkv_ref.at[:, n] for n in range(3))
    dq_ref, dk_ref, dv_ref = (out_ref.at[:, n] for n in range(3))

    @pl.loop(0, units, unroll=2)
    def _(t):
        for half in range(2):
            kt_ref[half * units + t] = rows_of(k_ref, half, t)[...].T
            dk_acc[half * units + t] = jnp.zeros((TILE, TILE), F32)
            dv_acc[half * units + t] = jnp.zeros((TILE, TILE), F32)

    for load in loads:
        load.wait()

    @pl.loop(0, units // multi)
    def _(step):
        plans = [[slot_plan(place_ref, tiles_ref, counts_ref, step * multi + u, j, units, width) for j in range(slots)] for u in range(multi)]
        zero = jnp.zeros((TILE, TILE), BF16)
        deltas, lses = [], []
        for u in range(multi):
            unit = step * multi + u
            delta, lse = [], []
            for half in range(2):
                prod = rows_of(g_ref, half, unit)[...].astype(F32) * rows_of(a_ref, half, unit)[...].astype(F32)
                delta.append(jnp.sum(prod.T, axis=0, keepdims=True))
                lse.append(lse_ref[half * units + unit][0:1])
            deltas.append(delta)
            lses.append(lse)
            for j, (in_first, half, tile) in enumerate(plans[u]):
                s_ref[u * slots + j] = mm(rows_of(k_ref, half, tile)[...], rows_of(q_ref, half, unit)[...], NT)
                dp_ref[u * slots + j] = mm(rows_of(v_ref, half, tile)[...], rows_of(g_ref, half, unit)[...], NT)
        for u in range(multi):
            for j, (in_first, half, tile) in enumerate(plans[u]):
                p = jnp.exp2(s_ref[u * slots + j] * scale2 - jnp.where(in_first, lses[u][0], lses[u][1]))
                ds = (p * (dp_ref[u * slots + j] - jnp.where(in_first, deltas[u][0], deltas[u][1]))).astype(BF16)
                p_ref[u * slots + j] = p.astype(BF16)
                d_ref[u, pl.ds(j * TILE, TILE), 0:TILE] = jnp.where(in_first, ds, zero)
                d_ref[u, pl.ds(j * TILE, TILE), TILE : 2 * TILE] = jnp.where(in_first, zero, ds)
        for u in range(multi):
            unit = step * multi + u
            for j, (in_first, half, tile) in enumerate(plans[u]):
                ds = d_ref[u, pl.ds(j * TILE, TILE), pl.ds(pl.multiple_of(half * TILE, TILE), TILE)]
                dv_acc[half * units + tile] += mm(p_ref[u * slots + j], rows_of(g_ref, half, unit)[...])
                dk_acc[half * units + tile] += mm(ds, rows_of(q_ref, half, unit)[...])
            kt = jnp.concatenate([kt_ref[half * units + tile] for _, half, tile in plans[u]], axis=1)
            dq_t = mm(kt, d_ref[u]) * scale
            for half in range(2):
                rows_of(dq_ref, half, unit)[...] = dq_t[:, half * TILE : (half + 1) * TILE].T.astype(BF16)

    @pl.loop(0, units, unroll=2)
    def _(t):
        for half in range(2):
            rows_of(dk_ref, half, t)[...] = (dk_acc[half * units + t] * scale).astype(BF16)
            rows_of(dv_ref, half, t)[...] = dv_acc[half * units + t].astype(BF16)


def attention_backward(place, tiles, counts, qkv, g, a, lse, after, width):
    seq, _, halves, tokens, head_dim = qkv.shape
    units = seq * tokens // TILE
    slots = width + 1
    return pl.pallas_call(
        functools.partial(backward_kernel, UNITS_AT_ONCE, slots, units, width, 1.0 / math.sqrt(head_dim)),
        out_shape=jax.ShapeDtypeStruct(qkv.shape, BF16),
        in_specs=[SMEM] * 3 + [VMEM] + [HBM] * (3 + len(after)),
        out_specs=VMEM,
        scratch_shapes=[
            pltpu.VMEM((halves * units, head_dim, TILE), BF16),
            pltpu.VMEM((halves * units, TILE, head_dim), F32),
            pltpu.VMEM((halves * units, TILE, head_dim), F32),
            pltpu.VMEM((UNITS_AT_ONCE * slots, TILE, TILE), F32),
            pltpu.VMEM((UNITS_AT_ONCE * slots, TILE, TILE), F32),
            pltpu.VMEM((UNITS_AT_ONCE * slots, TILE, TILE), BF16),
            pltpu.VMEM((UNITS_AT_ONCE, slots * TILE, 2 * TILE), BF16),
            pltpu.VMEM(g.shape, g.dtype),
            pltpu.VMEM(a.shape, a.dtype),
            pltpu.VMEM(lse.shape, lse.dtype),
            pltpu.SemaphoreType.DMA((3,)),
        ],
        compiler_params=pltpu.CompilerParams(vmem_limit_bytes=VMEM_LIMIT),
        cost_estimate=cost(3*10**11, MIB),
        name="attention_backward",
    )(place, tiles, counts, qkv, g, a, lse, *after)


def block_row(place_ref, side, ky, kz):
    y = lax.rem(place_ref[3] + side - ky, side)
    z = lax.rem(place_ref[4] + side - kz, side)
    return pl.multiple_of((y * side + z) * TILE, TILE)


def grad_attn_kernel(side, chips, place_ref, own_ref, other_ref, *refs):
    w_refs, g_ref = refs[: 2 * side], refs[-1]
    tokens = own_ref.shape[0]
    core = place_ref[2]
    for part in range(2):
        total = None
        for i in range(side):
            starts = [block_row(place_ref, side, *((i, j) if part == 0 else (j, i))) for j in range(side)]
            rows = [jnp.concatenate([ref[:, pl.ds(start, TILE)] for start in starts], axis=1) for ref in (own_ref, other_ref)]
            w = w_refs[part * side + i][...]
            step = mm(jnp.concatenate(rows, axis=0), w.reshape(side * TILE, w.shape[2]))
            total = step if total is None else total + step
        g = total.astype(BF16)
        for n in range(chips):
            x, half = divmod(part * chips + n, 2)
            for slot, first in ((core, 0), (1 - core, tokens)):
                target = pl.ds(pl.multiple_of(slot * tokens, tokens), tokens)
                g_ref[x, half, target, :] = g[first : first + tokens, n * TILE : (n + 1) * TILE]


def grad_attn(place, own, other, weights, after, side, chips):
    tokens, depth = own.shape
    columns = 2 * weights[0].shape[2]
    return pl.pallas_call(
        functools.partial(grad_attn_kernel, side, chips),
        out_shape=jax.ShapeDtypeStruct((chips, 2, 2 * tokens, TILE), BF16),
        in_specs=[SMEM] + [VMEM] * (2 + len(weights)) + [HBM],
        out_specs=VMEM,
        compiler_params=pltpu.CompilerParams(vmem_limit_bytes=VMEM_LIMIT),
        cost_estimate=cost(4 * tokens * depth * columns, 7 * MIB),
        name="grad_attn",
    )(place, own, other, *weights, after)


def row_copies(place_ref, block_refs, rows_ref, sems):
    chips = len(block_refs)
    halves, rows, width = block_refs[-1].shape
    tokens = rows // 2
    core = place_ref[2]
    copies = []
    for k, ref in enumerate(block_refs):
        chip = lax.rem(place_ref[5] + chips - k, chips)
        if k == 0:
            ref = ref.at[chip]
        for half in range(halves):
            target = pl.ds(pl.multiple_of((chip * halves + half) * width, width), width)
            for slot, first in ((core, 0), (1 - core, tokens)):
                source = ref.at[half, pl.ds(pl.multiple_of(slot * tokens, tokens), tokens), :]
                copies.append(pltpu.make_async_copy(source, rows_ref.at[pl.ds(first, tokens), target], sems.at[len(copies)]))
    return copies


def project_kernel(side, place_ref, *refs):
    block_refs, w_refs, (own_ref, other_ref, rows_ref, sems) = refs[: -5 - 2 * side], refs[-5 - 2 * side : -5], refs[-4:]
    copies = row_copies(place_ref, block_refs, rows_ref, sems)
    for copy in copies:
        copy.start()
    for copy in copies:
        copy.wait()
    tokens = own_ref.shape[0]
    for ky in range(side):
        for kz in range(0, side, 2):
            first = w_refs[ky][kz : kz + 2]
            second = jnp.concatenate([w_refs[side + kz][ky], w_refs[side + kz + 1][ky]], axis=0)
            w = jnp.concatenate([first.reshape(second.shape), second], axis=1)
            out = mm(rows_ref[...], w, NT)
            for n in range(2):
                target = pl.ds(block_row(place_ref, side, ky, kz + n), TILE)
                block = out[:, n * TILE : (n + 1) * TILE]
                own_ref[:, target] = block[:tokens]
                other_ref[:, target] = block[tokens:].astype(BF16)


def project(place, blocks, weights, after, side):
    features = side * side * weights[0].shape[1]
    columns = 2 * weights[0].shape[2]
    tokens = blocks[-1].shape[1] // 2
    return pl.pallas_call(
        functools.partial(project_kernel, side),
        out_shape=(jax.ShapeDtypeStruct((tokens, features), F32), jax.ShapeDtypeStruct((tokens, features), BF16)),
        in_specs=[SMEM] + [HBM] * len(blocks) + [VMEM] * len(weights) + [HBM],
        out_specs=(VMEM, VMEM),
        scratch_shapes=[pltpu.VMEM((2 * tokens, columns), BF16), pltpu.SemaphoreType.DMA((4 * len(blocks),))],
        compiler_params=pltpu.CompilerParams(vmem_limit_bytes=VMEM_LIMIT),
        cost_estimate=cost(4 * tokens * features * columns, 8 * MIB),
        name="project",
    )(place, *blocks, *weights, after)


def grad_weight_kernel(side, chips, place_ref, own_ref, other_ref, *refs):
    block_refs, out_refs, (rows_ref, grad_ref, part_ref, sems, load_sems) = refs[:chips], refs[chips:-5], refs[-5:]
    tokens = own_ref.shape[0]
    loads = row_copies(place_ref, block_refs, rows_ref, load_sems)
    for n, ref in enumerate((own_ref, other_ref)):
        target = grad_ref.at[pl.ds(n * tokens, tokens), :]
        loads.append(pltpu.make_async_copy(ref, target, load_sems.at[len(loads)]))
    for load in loads:
        load.start()
    for load in loads:
        load.wait()
    rows = part_ref.shape[2]
    half = part_ref.shape[3]
    copies = [pltpu.make_async_copy(part_ref.at[n], out_refs[n], sems.at[n]) for n in range(2 * side)]
    for ky in range(side):
        for kz in range(side):
            row = lax.rem(place_ref[3] + ky, side) * side + lax.rem(place_ref[4] + kz, side)
            columns = pl.ds(pl.multiple_of(row * rows, rows), rows)
            part = mm(grad_ref[:, columns], rows_ref[...], TN)
            part_ref[kz, ky] = part[:, :half].astype(BF16)
            part_ref[side + ky, kz] = part[:, half:].astype(BF16)
            if ky == side - 1:
                copies[kz].start()
        copies[side + ky].start()
    for copy in copies:
        copy.wait()


def grad_weight_parts(place, own, other, blocks, side):
    tokens, features = own.shape
    chips = len(blocks)
    columns = chips * blocks[-1].shape[0] * blocks[-1].shape[2]
    rows = features // side**2
    return pl.pallas_call(
        functools.partial(grad_weight_kernel, side, chips),
        out_shape=(jax.ShapeDtypeStruct((side, rows, columns // 2), BF16),) * (2 * side),
        in_specs=[SMEM] + [HBM] * (2 + chips),
        out_specs=(HBM,) * (2 * side),
        scratch_shapes=[
            pltpu.VMEM((2 * tokens, columns), BF16),
            pltpu.VMEM((2 * tokens, features), BF16),
            pltpu.VMEM((2 * side, side, rows, columns // 2), BF16),
            pltpu.SemaphoreType.DMA((2 * side,)),
            pltpu.SemaphoreType.DMA((4 * chips + 2,)),
        ],
        compiler_params=pltpu.CompilerParams(vmem_limit_bytes=VMEM_LIMIT),
        cost_estimate=cost(4 * tokens * features * columns, 7 * MIB),
        name="grad_weight_parts",
    )(place, own, other, *blocks)


def gate_kernel(*refs):
    del refs


def gate(values, *after):
    return pl.pallas_call(
        gate_kernel,
        out_shape=jax.ShapeDtypeStruct(values.shape, values.dtype),
        in_specs=[HBM] * (1 + len(after)),
        out_specs=HBM,
        input_output_aliases={0: 0},
        compiler_params=pltpu.CompilerParams(vmem_limit_bytes=VMEM_LIMIT),
        name="gate",
    )(values, *after)


def sum_kernel(*refs):
    side = len(refs) // 4
    for n in range(2):
        in_refs = refs[n * side : (n + 1) * side]
        for k in range(side):
            total = in_refs[0][k].astype(F32)
            for ref in in_refs[1:]:
                total = total + ref[k].astype(F32)
            refs[2 * side + n * side + k][...] = total.astype(BF16)


def summed(first, second):
    side, rows, width = first[0].shape
    sums = pl.pallas_call(
        sum_kernel,
        out_shape=(jax.ShapeDtypeStruct((rows, width), BF16),) * (2 * side),
        in_specs=[VMEM] * (2 * side),
        out_specs=(VMEM,) * (2 * side),
        compiler_params=pltpu.CompilerParams(vmem_limit_bytes=VMEM_LIMIT),
        cost_estimate=cost(10**12, MIB),
        name="summed",
    )(*first, *second)
    return sums[:side], sums[side:]


def sum_pair_kernel(*refs):
    out_ref = refs[-1]
    count = len(refs) // 2
    width = refs[0].shape[1]
    for side in range(2):
        total = refs[side * count][...].astype(F32)
        for ref in refs[side * count + 1 : (side + 1) * count]:
            total = total + ref[...].astype(F32)
        out_ref[:, side * width : (side + 1) * width] = total.astype(BF16)


def summed_side_by_side(first, second):
    rows, width = first[0].shape
    return pl.pallas_call(
        sum_pair_kernel,
        out_shape=jax.ShapeDtypeStruct((rows, 2 * width), BF16),
        in_specs=[VMEM] * (2 * len(first)),
        out_specs=VMEM,
        compiler_params=pltpu.CompilerParams(vmem_limit_bytes=VMEM_LIMIT),
        cost_estimate=cost(0, 4 * (len(first) + 1) * rows * width),
        name="summed_side_by_side",
    )(*first, *second)


def sum_chips_kernel(a_ref, b_ref, c_ref, d_ref, *refs):
    first = a_ref[...].astype(F32) + b_ref[...].astype(F32)
    second = c_ref[...].astype(F32) + d_ref[...].astype(F32)
    refs[-1][...] = (first + second).astype(BF16)


def summed_over_chips(parts, after):
    return pl.pallas_call(
        sum_chips_kernel,
        out_shape=jax.ShapeDtypeStruct(parts[0].shape, BF16),
        in_specs=[VMEM] * len(parts) + [HBM] * len(after),
        out_specs=VMEM,
        compiler_params=pltpu.CompilerParams(vmem_limit_bytes=VMEM_LIMIT),
        cost_estimate=cost(0, 10 * math.prod(parts[0].shape)),
        name="summed_over_chips",
    )(*parts, *after)


def per_device(queries, key_states, value_states, grad_output, out_weight, key_tiles, tile_count):
    seq = lax.axis_size("seq")
    ranks = lax.axis_size("dp")
    side = math.isqrt(ranks)
    chips = seq // 2
    s_index = lax.axis_index("seq")
    d_index = lax.axis_index("dp")
    core = lax.rem(s_index, 2)
    tokens, columns = queries.shape[1:]
    heads, units, width = key_tiles.shape[1:]
    head_dim = columns // heads
    rows = out_weight.shape[0]
    place = jnp.stack([s_index, jnp.int32(seq), core, lax.div(d_index, side), lax.rem(d_index, side), lax.div(s_index, 2)]).astype(jnp.int32)
    lists = key_tiles.reshape(-1)
    counts = tile_count.reshape(-1)
    same_core = [list(range(c, seq, 2)) for c in range(2)]
    across = [(i, i ^ 1) for i in range(seq)]

    def y_shift(k):
        return [(i, (i // side + k) % side * side + i % side) for i in range(ranks)]

    def z_shift(k):
        return [(i, i // side * side + (i % side + k) % side) for i in range(ranks)]

    def x_shift(k):
        return [(i, (i + 2 * k) % seq) for i in range(seq)]

    def x_swap(k):
        return [(i, i ^ (2 * k)) for i in range(seq)]

    def over_chips(values):
        return lax.all_to_all(values, "seq", split_axis=0, concat_axis=0, tiled=True, axis_index_groups=same_core)

    shard_z, shard_y = pack_weight(place, out_weight, chips)
    lines_z, lines_y = stack_lines(
        [shard_z] + [lax.ppermute(shard_z, "dp", z_shift(k)) for k in range(1, side)],
        [shard_y] + [lax.ppermute(shard_y, "dp", y_shift(k)) for k in range(1, side)],
    )
    weights = [lines_z] + [lax.ppermute(lines_z, "dp", y_shift(k)) for k in range(1, side)]
    weights += [lines_y] + [lax.ppermute(lines_y, "dp", z_shift(k)) for k in range(1, side)]
    packed = pack(queries, key_states, value_states, seq, head_dim)
    qkv = lax.all_to_all(packed, "seq", split_axis=0, concat_axis=0, tiled=True)
    own_rows = grad_output[0]
    other_rows = lax.ppermute(own_rows, "seq", across)
    a, lse, *a_blocks = attention_forward(place, lists, counts, qkv, chips, width)
    a_home = [a] + [lax.ppermute(a_blocks[k - 1], "seq", x_shift(k)) for k in range(1, chips)]
    g = over_chips(gate(grad_attn(place, own_rows, other_rows, weights, lse, side, chips), *a_home[1:]))
    parts = grad_weight_parts(place, own_rows, other_rows, a_home, side)
    z_first = [parts[0]] + [lax.ppermute(parts[k], "dp", z_shift(k)) for k in range(1, side)]
    y_first = [parts[side]] + [lax.ppermute(parts[side + k], "dp", y_shift(k)) for k in (1, side - 1)]
    grads = attention_backward(place, lists, counts, qkv, g, a, lse, (parts[0],), width)
    grads_home = lax.all_to_all(grads, "seq", split_axis=0, concat_axis=0, tiled=True)
    y_first += [lax.ppermute(gate(parts[side + k], grads), "dp", y_shift(k)) for k in range(2, side - 1)]

    z_sum, y_sum = summed(z_first, y_first)
    out_own, out_other = project(place, a_home, weights, grads, side)
    output = (out_own + lax.ppermute(out_other, "seq", across).astype(F32)).astype(BF16)
    chip_share = summed_side_by_side(
        [z_sum[0]] + [lax.ppermute(z_sum[k], "dp", y_shift(k)) for k in range(1, side)],
        [y_sum[0]] + [lax.ppermute(y_sum[k], "dp", z_shift(k)) for k in range(1, side)],
    )
    grad_query, grad_key, grad_value = unpack(grads_home)
    by_chip = [chip_share] + [lax.ppermute(chip_share, "seq", x_swap(k)) for k in range(1, chips)]
    own_half = summed_over_chips(by_chip, (grad_query, output))
    grad_weight = unpack_weight(place, own_half, lax.ppermute(own_half, "seq", across), chips)
    return output[None], grad_query, grad_key, grad_value, grad_weight


def solution(mesh):
    in_specs = (
        P("dp", "seq", None),
        P("dp", "seq", None),
        P("dp", "seq", None),
        P("dp", "seq", None),
        P("dp", None),
        P("dp", None, None, None),
        P("dp", None, None),
    )
    out_specs = (
        P("dp", "seq", None),
        P("dp", "seq", None),
        P("dp", "seq", None),
        P("dp", "seq", None),
        P("dp", None),
    )
    return jax.shard_map(per_device, mesh=mesh, in_specs=in_specs, out_specs=out_specs, check_vma=False)
```

```python
import functools
import math

import jax
import jax.numpy as jnp
from jax import lax
from jax.experimental import pallas as pl
from jax.experimental.pallas import tpu as pltpu
from jax.sharding import PartitionSpec as P

NN = (((1,), (0,)), ((), ()))
NT = (((1,), (1,)), ((), ()))
TN = (((0,), (0,)), ((), ()))
F32 = jnp.float32
BF16 = jnp.bfloat16
MIB = 2**20
SMEM = pl.BlockSpec(memory_space=pltpu.SMEM)
VMEM = pl.BlockSpec(memory_space=pltpu.VMEM)
ANY = pl.BlockSpec(memory_space=pl.ANY)
HBM = pl.BlockSpec(memory_space=pltpu.HBM)
TILE = 128
UNITS_AT_ONCE = 8
VMEM_LIMIT = 60 * MIB


def mm(a, b, dims=NN):
    return lax.dot_general(a, b, dims, preferred_element_type=F32)


def cost(flops, moved, exps=0):
    return pl.CostEstimate(flops=flops, bytes_accessed=moved, transcendentals=exps)


def pack_kernel(q_ref, k_ref, v_ref, out_ref, rows_ref, in_sems, out_sems):
    seq, _, halves, _, width = out_ref.shape
    loads = [pltpu.make_async_copy(ref.at[0], rows_ref.at[n], in_sems.at[n]) for n, ref in enumerate((q_ref, k_ref, v_ref))]
    for load in loads:
        load.start()
    stores = []
    for n, load in enumerate(loads):
        load.wait()
        for s in range(seq):
            for half in range(halves):
                source = rows_ref.at[n, :, pl.ds((s + seq * half) * width, width)]
                stores.append(pltpu.make_async_copy(source, out_ref.at[s, n, half], out_sems.at[len(stores)]))
                stores[-1].start()
    for store in stores:
        store.wait()


def pack(q, k, v, seq, head_dim):
    _, tokens, columns = q.shape
    halves = columns // (seq * head_dim)
    return pl.pallas_call(
        pack_kernel,
        out_shape=jax.ShapeDtypeStruct((seq, 3, halves, tokens, head_dim), q.dtype),
        in_specs=[HBM] * 3,
        out_specs=HBM,
        scratch_shapes=[
            pltpu.VMEM((3, tokens, columns), q.dtype),
            pltpu.SemaphoreType.DMA((3,)),
            pltpu.SemaphoreType.DMA((3 * seq * halves,)),
        ],
        compiler_params=pltpu.CompilerParams(vmem_limit_bytes=VMEM_LIMIT),
        cost_estimate=cost(0, 12 * tokens * columns),
        name="pack_heads",
    )(q, k, v)


def unpack_kernel(in_ref, q_ref, k_ref, v_ref):
    seq, _, halves, _, width = in_ref.shape
    for n, ref in enumerate((q_ref, k_ref, v_ref)):
        for s in range(seq):
            for half in range(halves):
                column = (s + seq * half) * width
                ref[0, :, column : column + width] = in_ref[s, n, half]


def unpack(blocks):
    seq, _, halves, tokens, head_dim = blocks.shape
    columns = seq * halves * head_dim
    rows = tokens // 4
    return pl.pallas_call(
        unpack_kernel,
        grid=(tokens // rows,),
        out_shape=(jax.ShapeDtypeStruct((1, tokens, columns), blocks.dtype),) * 3,
        in_specs=[pl.BlockSpec((seq, 3, halves, rows, head_dim), lambda i: (0, 0, 0, i, 0))],
        out_specs=(pl.BlockSpec((1, rows, columns), lambda i: (0, i, 0)),) * 3,
        compiler_params=pltpu.CompilerParams(vmem_limit_bytes=VMEM_LIMIT),
        cost_estimate=cost(0, 12 * tokens * columns),
        name="unpack_heads",
    )(blocks)


def core_columns(core, chips):
    return [pl.multiple_of((2 * x + core + 2 * chips * half) * TILE, TILE) for x in range(chips) for half in range(2)]


def pack_weight_kernel(chips, place_ref, in_ref, *out_refs):
    for i, column in enumerate(core_columns(place_ref[2], chips)):
        out_refs[i // chips][:, pl.ds(i % chips * TILE, TILE)] = in_ref[:, pl.ds(column, TILE)]


def pack_weight(place, shard, chips):
    rows, columns = shard.shape
    return pl.pallas_call(
        functools.partial(pack_weight_kernel, chips),
        out_shape=(jax.ShapeDtypeStruct((rows, columns // 4), shard.dtype),) * 2,
        in_specs=[SMEM, VMEM],
        out_specs=(VMEM,) * 2,
        compiler_params=pltpu.CompilerParams(vmem_limit_bytes=VMEM_LIMIT),
        cost_estimate=cost(0, 3 * rows * columns),
        name="pack_weight",
    )(place, shard)


def stack_kernel(*refs):
    count = len(refs) // 2 - 1
    for n in range(2):
        for k in range(count):
            refs[2 * count + n][k] = refs[n * count + k][...]


def stack_lines(first, second):
    shape = (len(first), *first[0].shape)
    return pl.pallas_call(
        stack_kernel,
        out_shape=(jax.ShapeDtypeStruct(shape, first[0].dtype),) * 2,
        in_specs=[VMEM] * (2 * len(first)),
        out_specs=(VMEM,) * 2,
        compiler_params=pltpu.CompilerParams(vmem_limit_bytes=VMEM_LIMIT),
        cost_estimate=cost(0, 8 * math.prod(shape)),
        name="stack_lines",
    )(*first, *second)


def unpack_weight_kernel(chips, place_ref, own_ref, other_ref, out_ref):
    for ref, core in ((own_ref, place_ref[2]), (other_ref, 1 - place_ref[2])):
        for i, column in enumerate(core_columns(core, chips)):
            out_ref[:, pl.ds(column, TILE)] = ref[:, pl.ds(i * TILE, TILE)].astype(F32)


def unpack_weight(place, own, other, chips):
    rows, columns = own.shape
    return pl.pallas_call(
        functools.partial(unpack_weight_kernel, chips),
        out_shape=jax.ShapeDtypeStruct((rows, 2 * columns), F32),
        in_specs=[SMEM, VMEM, VMEM],
        out_specs=VMEM,
        compiler_params=pltpu.CompilerParams(vmem_limit_bytes=VMEM_LIMIT),
        cost_estimate=cost(0, 12 * rows * columns),
        name="unpack_weight",
    )(place, own, other)


def slot_plan(place_ref, tiles_ref, counts_ref, unit, slot, units, width):
    first_head = place_ref[0]
    split = counts_ref[first_head * units + unit]
    in_first = slot < split
    head = jnp.where(in_first, first_head, first_head + place_ref[1])
    entry = jnp.minimum(jnp.where(in_first, slot, width - slot), width - 1)
    tile = tiles_ref[(head * units + unit) * width + entry]
    return in_first, jnp.where(in_first, 0, 1), tile


def rows_of(ref, half, tile):
    per_block = ref.shape[2] // TILE
    start = pl.multiple_of(lax.rem(tile, per_block) * TILE, TILE)
    return ref.at[lax.div(tile, per_block), half, pl.ds(start, TILE), :]


def forward_kernel(multi, slots, units, width, scale, place_ref, tiles_ref, counts_ref, qkv_ref, a_ref, lse_ref, *refs):
    block_refs, (vt_ref, s_ref, p_ref) = refs[:-3], refs[-3:]
    scale2 = scale * math.log2(math.e)
    q_ref, k_ref, v_ref = (qkv_ref.at[:, n] for n in range(3))

    @pl.loop(0, units, unroll=2)
    def _(t):
        for half in range(2):
            vt_ref[half * units + t] = rows_of(v_ref, half, t)[...].T

    @pl.loop(0, units // multi)
    def _(step):
        plans = [[slot_plan(place_ref, tiles_ref, counts_ref, step * multi + u, j, units, width) for j in range(slots)] for u in range(multi)]
        all_tops = []
        for u in range(multi):
            tops = []
            for j, (in_first, half, tile) in enumerate(plans[u]):
                s = mm(rows_of(k_ref, half, tile)[...], rows_of(q_ref, half, step * multi + u)[...], NT)
                s_ref[u * slots + j] = s
                tops.append(jnp.max(s.reshape(TILE // 8, 8, TILE), axis=0))
            all_tops.append(tops)
        low = jnp.full((8, TILE), -jnp.inf, F32)
        zero = jnp.zeros((TILE, TILE), BF16)
        stats = []
        for u in range(multi):
            top = []
            for half in range(2):
                m = low
                for (in_first, _, _), t8 in zip(plans[u], all_tops[u]):
                    use = in_first if half == 0 else jnp.logical_not(in_first)
                    m = jnp.maximum(m, jnp.where(use, t8, low))
                top.append(jnp.max(m, axis=0, keepdims=True) * scale2)
            totals = [jnp.zeros((8, TILE), F32)] * 2
            for j, (in_first, half, tile) in enumerate(plans[u]):
                p = jnp.exp2(s_ref[u * slots + j] * scale2 - jnp.where(in_first, top[0], top[1]))
                l8 = jnp.sum(p.reshape(TILE // 8, 8, TILE), axis=0)
                totals[0] = totals[0] + jnp.where(in_first, l8, 0.0)
                totals[1] = totals[1] + jnp.where(in_first, 0.0, l8)
                pb = p.astype(BF16)
                p_ref[u, pl.ds(j * TILE, TILE), 0:TILE] = jnp.where(in_first, pb, zero)
                p_ref[u, pl.ds(j * TILE, TILE), TILE : 2 * TILE] = jnp.where(in_first, zero, pb)
            stats.append((top, totals))
        for u in range(multi):
            unit = step * multi + u
            top, totals = stats[u]
            vt = jnp.concatenate([vt_ref[half * units + tile] for _, half, tile in plans[u]], axis=1)
            mixed = mm(vt, p_ref[u])
            for half in range(2):
                total = jnp.sum(totals[half], axis=0, keepdims=True)
                a_t = mixed[:, half * TILE : (half + 1) * TILE] / total
                rows_of(a_ref, half, unit)[...] = a_t.T.astype(BF16)
                lse_ref[half * units + unit] = jnp.broadcast_to(top[half] + jnp.log2(total), (8, TILE))

    chips = len(block_refs) + 1
    for k, ref in enumerate(block_refs, 1):
        ref[...] = a_ref[lax.rem(place_ref[5] + k, chips)]


def attention_forward(place, tiles, counts, qkv, chips, width):
    seq, _, halves, tokens, head_dim = qkv.shape
    units = seq * tokens // TILE
    slots = width + 1
    rows = seq * tokens // chips
    return pl.pallas_call(
        functools.partial(forward_kernel, UNITS_AT_ONCE, slots, units, width, 1.0 / math.sqrt(head_dim)),
        out_shape=(
            jax.ShapeDtypeStruct((chips, halves, rows, head_dim), BF16),
            jax.ShapeDtypeStruct((halves * units, 8, TILE), F32),
        )
        + (jax.ShapeDtypeStruct((halves, rows, head_dim), BF16),) * (chips - 1),
        in_specs=[SMEM] * 3 + [VMEM],
        out_specs=(VMEM,) * (1 + chips),
        scratch_shapes=[
            pltpu.VMEM((halves * units, head_dim, TILE), BF16),
            pltpu.VMEM((UNITS_AT_ONCE * slots, TILE, TILE), F32),
            pltpu.VMEM((UNITS_AT_ONCE, slots * TILE, 2 * TILE), BF16),
        ],
        compiler_params=pltpu.CompilerParams(vmem_limit_bytes=28 * MIB),
        cost_estimate=cost(3*10**11, MIB),
        name="attention_forward",
    )(place, tiles, counts, qkv)


def backward_kernel(multi, slots, units, width, scale, place_ref, tiles_ref, counts_ref, qkv_ref, g_ref, a_ref, lse_ref, *refs):
    out_ref, kt_ref, dk_acc, dv_acc, s_ref, dp_ref, p_ref, d_ref = refs[-12:-4]
    loads = [pltpu.make_async_copy(ref, refs[n - 4], refs[-1].at[n]) for n, ref in enumerate((g_ref, a_ref, lse_ref))]
    for load in loads:
        load.start()
    g_ref, a_ref, lse_ref = refs[-4:-1]
    scale2 = scale * math.log2(math.e)
    q_ref, k_ref, v_ref = (qkv_ref.at[:, n] for n in range(3))
    dq_ref, dk_ref, dv_ref = (out_ref.at[:, n] for n in range(3))

    @pl.loop(0, units, unroll=2)
    def _(t):
        for half in range(2):
            kt_ref[half * units + t] = rows_of(k_ref, half, t)[...].T
            dk_acc[half * units + t] = jnp.zeros((TILE, TILE), F32)
            dv_acc[half * units + t] = jnp.zeros((TILE, TILE), F32)

    for load in loads:
        load.wait()

    @pl.loop(0, units // multi)
    def _(step):
        plans = [[slot_plan(place_ref, tiles_ref, counts_ref, step * multi + u, j, units, width) for j in range(slots)] for u in range(multi)]
        zero = jnp.zeros((TILE, TILE), BF16)
        deltas, lses = [], []
        for u in range(multi):
            unit = step * multi + u
            delta, lse = [], []
            for half in range(2):
                prod = rows_of(g_ref, half, unit)[...].astype(F32) * rows_of(a_ref, half, unit)[...].astype(F32)
                delta.append(jnp.sum(prod.T, axis=0, keepdims=True))
                lse.append(lse_ref[half * units + unit][0:1])
            deltas.append(delta)
            lses.append(lse)
            for j, (in_first, half, tile) in enumerate(plans[u]):
                s_ref[u * slots + j] = mm(rows_of(k_ref, half, tile)[...], rows_of(q_ref, half, unit)[...], NT)
                dp_ref[u * slots + j] = mm(rows_of(v_ref, half, tile)[...], rows_of(g_ref, half, unit)[...], NT)
        for u in range(multi):
            for j, (in_first, half, tile) in enumerate(plans[u]):
                p = jnp.exp2(s_ref[u * slots + j] * scale2 - jnp.where(in_first, lses[u][0], lses[u][1]))
                ds = (p * (dp_ref[u * slots + j] - jnp.where(in_first, deltas[u][0], deltas[u][1]))).astype(BF16)
                p_ref[u * slots + j] = p.astype(BF16)
                d_ref[u, pl.ds(j * TILE, TILE), 0:TILE] = jnp.where(in_first, ds, zero)
                d_ref[u, pl.ds(j * TILE, TILE), TILE : 2 * TILE] = jnp.where(in_first, zero, ds)
        for u in range(multi):
            unit = step * multi + u
            for j, (in_first, half, tile) in enumerate(plans[u]):
                ds = d_ref[u, pl.ds(j * TILE, TILE), pl.ds(pl.multiple_of(half * TILE, TILE), TILE)]
                dv_acc[half * units + tile] += mm(p_ref[u * slots + j], rows_of(g_ref, half, unit)[...])
                dk_acc[half * units + tile] += mm(ds, rows_of(q_ref, half, unit)[...])
            kt = jnp.concatenate([kt_ref[half * units + tile] for _, half, tile in plans[u]], axis=1)
            dq_t = mm(kt, d_ref[u]) * scale
            for half in range(2):
                rows_of(dq_ref, half, unit)[...] = dq_t[:, half * TILE : (half + 1) * TILE].T.astype(BF16)

    @pl.loop(0, units, unroll=2)
    def _(t):
        for half in range(2):
            rows_of(dk_ref, half, t)[...] = (dk_acc[half * units + t] * scale).astype(BF16)
            rows_of(dv_ref, half, t)[...] = dv_acc[half * units + t].astype(BF16)


def attention_backward(place, tiles, counts, qkv, g, a, lse, after, width):
    seq, _, halves, tokens, head_dim = qkv.shape
    units = seq * tokens // TILE
    slots = width + 1
    return pl.pallas_call(
        functools.partial(backward_kernel, UNITS_AT_ONCE, slots, units, width, 1.0 / math.sqrt(head_dim)),
        out_shape=jax.ShapeDtypeStruct(qkv.shape, BF16),
        in_specs=[SMEM] * 3 + [VMEM] + [HBM] * (3 + len(after)),
        out_specs=VMEM,
        scratch_shapes=[
            pltpu.VMEM((halves * units, head_dim, TILE), BF16),
            pltpu.VMEM((halves * units, TILE, head_dim), F32),
            pltpu.VMEM((halves * units, TILE, head_dim), F32),
            pltpu.VMEM((UNITS_AT_ONCE * slots, TILE, TILE), F32),
            pltpu.VMEM((UNITS_AT_ONCE * slots, TILE, TILE), F32),
            pltpu.VMEM((UNITS_AT_ONCE * slots, TILE, TILE), BF16),
            pltpu.VMEM((UNITS_AT_ONCE, slots * TILE, 2 * TILE), BF16),
            pltpu.VMEM(g.shape, g.dtype),
            pltpu.VMEM(a.shape, a.dtype),
            pltpu.VMEM(lse.shape, lse.dtype),
            pltpu.SemaphoreType.DMA((3,)),
        ],
        compiler_params=pltpu.CompilerParams(vmem_limit_bytes=VMEM_LIMIT),
        cost_estimate=cost(3*10**11, MIB),
        name="attention_backward",
    )(place, tiles, counts, qkv, g, a, lse, *after)


def block_row(place_ref, side, ky, kz):
    y = lax.rem(place_ref[3] + side - ky, side)
    z = lax.rem(place_ref[4] + side - kz, side)
    return pl.multiple_of((y * side + z) * TILE, TILE)


def grad_attn_kernel(side, chips, place_ref, own_ref, other_ref, *refs):
    w_refs, g_ref = refs[: 2 * side], refs[-1]
    tokens = own_ref.shape[0]
    core = place_ref[2]
    for part in range(2):
        total = None
        for i in range(side):
            starts = [block_row(place_ref, side, *((i, j) if part == 0 else (j, i))) for j in range(side)]
            rows = [jnp.concatenate([ref[:, pl.ds(start, TILE)] for start in starts], axis=1) for ref in (own_ref, other_ref)]
            w = w_refs[part * side + i][...]
            step = mm(jnp.concatenate(rows, axis=0), w.reshape(side * TILE, w.shape[2]))
            total = step if total is None else total + step
        g = total.astype(BF16)
        for n in range(chips):
            x, half = divmod(part * chips + n, 2)
            for slot, first in ((core, 0), (1 - core, tokens)):
                target = pl.ds(pl.multiple_of(slot * tokens, tokens), tokens)
                g_ref[x, half, target, :] = g[first : first + tokens, n * TILE : (n + 1) * TILE]


def grad_attn(place, own, other, weights, after, side, chips):
    tokens, depth = own.shape
    columns = 2 * weights[0].shape[2]
    return pl.pallas_call(
        functools.partial(grad_attn_kernel, side, chips),
        out_shape=jax.ShapeDtypeStruct((chips, 2, 2 * tokens, TILE), BF16),
        in_specs=[SMEM] + [VMEM] * (2 + len(weights)) + [HBM],
        out_specs=VMEM,
        compiler_params=pltpu.CompilerParams(vmem_limit_bytes=VMEM_LIMIT),
        cost_estimate=cost(4 * tokens * depth * columns, 7 * MIB),
        name="grad_attn",
    )(place, own, other, *weights, after)


def row_copies(place_ref, block_refs, rows_ref, sems):
    chips = len(block_refs)
    halves, rows, width = block_refs[-1].shape
    tokens = rows // 2
    core = place_ref[2]
    copies = []
    for k, ref in enumerate(block_refs):
        chip = lax.rem(place_ref[5] + chips - k, chips)
        if k == 0:
            ref = ref.at[chip]
        for half in range(halves):
            target = pl.ds(pl.multiple_of((chip * halves + half) * width, width), width)
            for slot, first in ((core, 0), (1 - core, tokens)):
                source = ref.at[half, pl.ds(pl.multiple_of(slot * tokens, tokens), tokens), :]
                copies.append(pltpu.make_async_copy(source, rows_ref.at[pl.ds(first, tokens), target], sems.at[len(copies)]))
    return copies


def project_kernel(side, place_ref, *refs):
    block_refs, w_refs, (own_ref, other_ref, rows_ref, sems) = refs[: -5 - 2 * side], refs[-5 - 2 * side : -5], refs[-4:]
    copies = row_copies(place_ref, block_refs, rows_ref, sems)
    for copy in copies:
        copy.start()
    for copy in copies:
        copy.wait()
    tokens = own_ref.shape[0]
    for ky in range(side):
        for kz in range(0, side, 2):
            first = w_refs[ky][kz : kz + 2]
            second = jnp.concatenate([w_refs[side + kz][ky], w_refs[side + kz + 1][ky]], axis=0)
            w = jnp.concatenate([first.reshape(second.shape), second], axis=1)
            out = mm(rows_ref[...], w, NT)
            for n in range(2):
                target = pl.ds(block_row(place_ref, side, ky, kz + n), TILE)
                block = out[:, n * TILE : (n + 1) * TILE]
                own_ref[:, target] = block[:tokens]
                other_ref[:, target] = block[tokens:].astype(BF16)


def project(place, blocks, weights, after, side):
    features = side * side * weights[0].shape[1]
    columns = 2 * weights[0].shape[2]
    tokens = blocks[-1].shape[1] // 2
    return pl.pallas_call(
        functools.partial(project_kernel, side),
        out_shape=(jax.ShapeDtypeStruct((tokens, features), F32), jax.ShapeDtypeStruct((tokens, features), BF16)),
        in_specs=[SMEM] + [HBM] * len(blocks) + [VMEM] * len(weights) + [HBM],
        out_specs=(VMEM, VMEM),
        scratch_shapes=[pltpu.VMEM((2 * tokens, columns), BF16), pltpu.SemaphoreType.DMA((4 * len(blocks),))],
        compiler_params=pltpu.CompilerParams(vmem_limit_bytes=VMEM_LIMIT),
        cost_estimate=cost(4 * tokens * features * columns, 8 * MIB),
        name="project",
    )(place, *blocks, *weights, after)


def grad_weight_kernel(side, chips, place_ref, own_ref, other_ref, *refs):
    block_refs, out_refs, (rows_ref, grad_ref, part_ref, sems, load_sems) = refs[:chips], refs[chips:-5], refs[-5:]
    tokens = own_ref.shape[0]
    loads = row_copies(place_ref, block_refs, rows_ref, load_sems)
    for n, ref in enumerate((own_ref, other_ref)):
        target = grad_ref.at[pl.ds(n * tokens, tokens), :]
        loads.append(pltpu.make_async_copy(ref, target, load_sems.at[len(loads)]))
    for load in loads:
        load.start()
    for load in loads:
        load.wait()
    rows = part_ref.shape[2]
    half = part_ref.shape[3]
    copies = [pltpu.make_async_copy(part_ref.at[n], out_refs[n], sems.at[n]) for n in range(2 * side)]
    for ky in range(side):
        for kz in range(side):
            row = lax.rem(place_ref[3] + ky, side) * side + lax.rem(place_ref[4] + kz, side)
            columns = pl.ds(pl.multiple_of(row * rows, rows), rows)
            part = mm(grad_ref[:, columns], rows_ref[...], TN)
            part_ref[kz, ky] = part[:, :half].astype(BF16)
            part_ref[side + ky, kz] = part[:, half:].astype(BF16)
            if ky == side - 1:
                copies[kz].start()
        copies[side + ky].start()
    for copy in copies:
        copy.wait()


def grad_weight_parts(place, own, other, blocks, side):
    tokens, features = own.shape
    chips = len(blocks)
    columns = chips * blocks[-1].shape[0] * blocks[-1].shape[2]
    rows = features // side**2
    return pl.pallas_call(
        functools.partial(grad_weight_kernel, side, chips),
        out_shape=(jax.ShapeDtypeStruct((side, rows, columns // 2), BF16),) * (2 * side),
        in_specs=[SMEM] + [HBM] * (2 + chips),
        out_specs=(HBM,) * (2 * side),
        scratch_shapes=[
            pltpu.VMEM((2 * tokens, columns), BF16),
            pltpu.VMEM((2 * tokens, features), BF16),
            pltpu.VMEM((2 * side, side, rows, columns // 2), BF16),
            pltpu.SemaphoreType.DMA((2 * side,)),
            pltpu.SemaphoreType.DMA((4 * chips + 2,)),
        ],
        compiler_params=pltpu.CompilerParams(vmem_limit_bytes=VMEM_LIMIT),
        cost_estimate=cost(4 * tokens * features * columns, 7 * MIB),
        name="grad_weight_parts",
    )(place, own, other, *blocks)


def gate_kernel(*refs):
    del refs


def gate(values, *after, weight=0):
    return pl.pallas_call(
        gate_kernel,
        out_shape=jax.ShapeDtypeStruct(values.shape, values.dtype),
        in_specs=[HBM] * (1 + len(after)),
        out_specs=HBM,
        input_output_aliases={0: 0},
        compiler_params=pltpu.CompilerParams(vmem_limit_bytes=VMEM_LIMIT),
        cost_estimate=cost(weight, 0),
        name="gate",
    )(values, *after)


def sum_kernel(*refs):
    side = len(refs) // 4
    for n in range(2):
        in_refs = refs[n * side : (n + 1) * side]
        for k in range(side):
            total = in_refs[0][k].astype(F32)
            for ref in in_refs[1:]:
                total = total + ref[k].astype(F32)
            refs[2 * side + n * side + k][...] = total.astype(BF16)


def summed(first, second):
    side, rows, width = first[0].shape
    sums = pl.pallas_call(
        sum_kernel,
        out_shape=(jax.ShapeDtypeStruct((rows, width), BF16),) * (2 * side),
        in_specs=[VMEM] * (2 * side),
        out_specs=(VMEM,) * (2 * side),
        compiler_params=pltpu.CompilerParams(vmem_limit_bytes=VMEM_LIMIT),
        cost_estimate=cost(10**12, MIB),
        name="summed",
    )(*first, *second)
    return sums[:side], sums[side:]


def sum_pair_kernel(*refs):
    out_ref = refs[-1]
    count = len(refs) // 2
    width = refs[0].shape[1]
    for side in range(2):
        total = refs[side * count][...].astype(F32)
        for ref in refs[side * count + 1 : (side + 1) * count]:
            total = total + ref[...].astype(F32)
        out_ref[:, side * width : (side + 1) * width] = total.astype(BF16)


def summed_side_by_side(first, second):
    rows, width = first[0].shape
    return pl.pallas_call(
        sum_pair_kernel,
        out_shape=jax.ShapeDtypeStruct((rows, 2 * width), BF16),
        in_specs=[VMEM] * (2 * len(first)),
        out_specs=VMEM,
        compiler_params=pltpu.CompilerParams(vmem_limit_bytes=VMEM_LIMIT),
        cost_estimate=cost(0, 4 * (len(first) + 1) * rows * width),
        name="summed_side_by_side",
    )(*first, *second)


def sum_chips_kernel(a_ref, b_ref, c_ref, d_ref, *refs):
    first = a_ref[...].astype(F32) + b_ref[...].astype(F32)
    second = c_ref[...].astype(F32) + d_ref[...].astype(F32)
    refs[-1][...] = (first + second).astype(BF16)


def summed_over_chips(parts, after):
    return pl.pallas_call(
        sum_chips_kernel,
        out_shape=jax.ShapeDtypeStruct(parts[0].shape, BF16),
        in_specs=[VMEM] * len(parts) + [HBM] * len(after),
        out_specs=VMEM,
        compiler_params=pltpu.CompilerParams(vmem_limit_bytes=VMEM_LIMIT),
        cost_estimate=cost(0, 10 * math.prod(parts[0].shape)),
        name="summed_over_chips",
    )(*parts, *after)


def per_device(queries, key_states, value_states, grad_output, out_weight, key_tiles, tile_count):
    seq = lax.axis_size("seq")
    ranks = lax.axis_size("dp")
    side = math.isqrt(ranks)
    chips = seq // 2
    s_index = lax.axis_index("seq")
    d_index = lax.axis_index("dp")
    core = lax.rem(s_index, 2)
    tokens, columns = queries.shape[1:]
    heads, units, width = key_tiles.shape[1:]
    head_dim = columns // heads
    rows = out_weight.shape[0]
    place = jnp.stack([s_index, jnp.int32(seq), core, lax.div(d_index, side), lax.rem(d_index, side), lax.div(s_index, 2)]).astype(jnp.int32)
    lists = key_tiles.reshape(-1)
    counts = tile_count.reshape(-1)
    same_core = [list(range(c, seq, 2)) for c in range(2)]
    across = [(i, i ^ 1) for i in range(seq)]

    def y_shift(k):
        return [(i, (i // side + k) % side * side + i % side) for i in range(ranks)]

    def z_shift(k):
        return [(i, i // side * side + (i % side + k) % side) for i in range(ranks)]

    def x_shift(k):
        return [(i, (i + 2 * k) % seq) for i in range(seq)]

    def x_swap(k):
        return [(i, i ^ (2 * k)) for i in range(seq)]

    def over_chips(values):
        return lax.all_to_all(values, "seq", split_axis=0, concat_axis=0, tiled=True, axis_index_groups=same_core)

    shard_z, shard_y = pack_weight(place, out_weight, chips)
    lines_z, lines_y = stack_lines(
        [shard_z] + [lax.ppermute(shard_z, "dp", z_shift(k)) for k in range(1, side)],
        [shard_y] + [lax.ppermute(shard_y, "dp", y_shift(k)) for k in range(1, side)],
    )
    weights = [lines_z] + [lax.ppermute(lines_z, "dp", y_shift(k)) for k in range(1, side)]
    weights += [lines_y] + [lax.ppermute(lines_y, "dp", z_shift(k)) for k in range(1, side)]
    packed = pack(queries, key_states, value_states, seq, head_dim)
    qkv = lax.all_to_all(packed, "seq", split_axis=0, concat_axis=0, tiled=True)
    own_rows = grad_output[0]
    other_rows = lax.ppermute(own_rows, "seq", across)
    a, lse, *a_blocks = attention_forward(place, lists, counts, qkv, chips, width)
    a_home = [a] + [lax.ppermute(a_blocks[k - 1], "seq", x_shift(k)) for k in range(1, chips)]
    g = over_chips(gate(grad_attn(place, own_rows, other_rows, weights, lse, side, chips), *a_home[1:]))
    parts = grad_weight_parts(place, own_rows, other_rows, a_home, side)
    z_first = [parts[0]] + [lax.ppermute(parts[k], "dp", z_shift(k)) for k in range(1, side)]
    y_first = [parts[side]] + [lax.ppermute(parts[side + k], "dp", y_shift(k)) for k in (1, side - 1)]
    grads = attention_backward(place, lists, counts, qkv, g, a, lse, (parts[0],), width)
    grads_home = lax.all_to_all(grads, "seq", split_axis=0, concat_axis=0, tiled=True)
    y_first += [lax.ppermute(gate(parts[side + k], grads, weight=10**12), "dp", y_shift(k)) for k in range(2, side - 1)]

    z_sum, y_sum = summed(z_first, y_first)
    out_own, out_other = project(place, a_home, weights, grads, side)
    output = (out_own + lax.ppermute(out_other, "seq", across).astype(F32)).astype(BF16)
    chip_share = summed_side_by_side(
        [z_sum[0]] + [lax.ppermute(z_sum[k], "dp", y_shift(k)) for k in range(1, side)],
        [y_sum[0]] + [lax.ppermute(y_sum[k], "dp", z_shift(k)) for k in range(1, side)],
    )
    grad_query, grad_key, grad_value = unpack(grads_home)
    by_chip = [chip_share] + [lax.ppermute(chip_share, "seq", x_swap(k)) for k in range(1, chips)]
    own_half = summed_over_chips(by_chip, (grad_query, output))
    grad_weight = unpack_weight(place, own_half, lax.ppermute(own_half, "seq", across), chips)
    return output[None], grad_query, grad_key, grad_value, grad_weight


def solution(mesh):
    in_specs = (
        P("dp", "seq", None),
        P("dp", "seq", None),
        P("dp", "seq", None),
        P("dp", "seq", None),
        P("dp", None),
        P("dp", None, None, None),
        P("dp", None, None),
    )
    out_specs = (
        P("dp", "seq", None),
        P("dp", "seq", None),
        P("dp", "seq", None),
        P("dp", "seq", None),
        P("dp", None),
    )
    return jax.shard_map(per_device, mesh=mesh, in_specs=in_specs, out_specs=out_specs, check_vma=False)
```
